512 devices in a mesh: pt: 32 (over z, core), ctr: 16 (over y, x).
Axes of the slice: x: 4, y: 4, z: 16, core: 2. Of those that a mesh axis runs over, the one named last changes fastest.
Arguments:
- points: bfloat16 [32768, 128], P('pt'), may hold values from -1.56 to 1.56
- centres: bfloat16 [65536, 128], P(('pt', 'ctr')), may hold values from -1.56 to 1.56
- factor: float32 [65536, 128], P(('pt', 'ctr')), as said below
- solution: float32 [65536, 64], P(('pt', 'ctr')), may hold values from -4 to 4
- residual: float32 [65536, 64], P(('pt', 'ctr')), may hold values from -6 to 6
- direction: float32 [65536, 64], P(('pt', 'ctr')), may hold values from -6 to 6
Outputs:
- solution_out: float32 [65536, 64], P(('pt', 'ctr'))
- residual_out: float32 [65536, 64], P(('pt', 'ctr'))
The draws below stay inside these ranges and needn't reach their ends.
Inputs may be any that keep to these rules, and one draw needn't show every extreme that they name: `factor`: each block of 128 rows is lower triangular with a diagonal between 1 and 2.
All inputs are finite; a program needn't handle non-finite values.
Results may differ from the reference program's by a relative error of at most 0.0046.
Values may be sent and summed in bfloat16 or wider, within the bound.
No kernel may reach another device: no remote copies, remote signals or barrier semaphores. Data moves between devices by JAX's collectives and lax.ppermute only.
A program may use at most 64 MiB of HBM per device.

```python
import math
import jax
import jax.numpy as jnp
from jax import lax

DIM = 128
OUTS = 64
CB = 128
PT_DEV = 1024
ITERS = 2
POINTS = 32768
CENTRES = 65536


def group_count():
    return 8 * (POINTS // PT_DEV)


def group_table(key, scale_low, scale_high):
    key = jax.random.fold_in(key, 5)
    key_phase, key_scale = jax.random.split(key)
    phases = jax.random.uniform(key_phase, (group_count(), DIM // 2), jnp.float32, -math.pi, math.pi)
    scales = jax.random.uniform(key_scale, (group_count(), 1), jnp.float32, scale_low, scale_high)
    return (phases, scales)


def grouped_rows(key, labels, phases, scales, spread, jitter):
    row_count = labels.shape[0]
    key_shift, key_radius = jax.random.split(key)
    shift = jax.random.uniform(key_shift, (row_count, DIM // 2), jnp.float32, -spread, spread)
    angle = jnp.take(phases, labels, axis=0) + shift
    radius_sq = jnp.take(scales, labels, axis=0) + jax.random.uniform(key_radius, (row_count, DIM // 2), jnp.float32, -jitter, jitter)
    radius = jnp.sqrt(radius_sq)
    paired = jnp.stack([radius * jnp.cos(angle), radius * jnp.sin(angle)], axis=2)
    return paired.reshape(row_count, DIM)


def draw_points(key, part):
    phases, scales = group_table(key, 1.8, 2.2)
    key = jax.random.fold_in(key, 11)
    key_label, key_rows = jax.random.split(key)
    owner = jnp.arange(POINTS, dtype=jnp.int32) // PT_DEV
    labels = 8 * owner + jax.random.randint(key_label, (POINTS,), 0, 8, jnp.int32)
    return grouped_rows(key_rows, labels, phases, scales, 1.8, 0.0).astype(jnp.bfloat16)


def draw_centres(key, part):
    phases, scales = group_table(key, 1.8, 2.2)
    key = jax.random.fold_in(key, 13)
    key_label, key_rows = jax.random.split(key)
    labels = jax.random.randint(key_label, (CENTRES,), 0, group_count(), jnp.int32)
    return grouped_rows(key_rows, labels, phases, scales, 1.8, 0.0).astype(jnp.bfloat16)


def draw_factor(key, part):
    key = jax.random.fold_in(key, 7)
    key_off, key_diag = jax.random.split(key)
    rows = jnp.arange(CENTRES)[:, None] % CB
    cols = jnp.arange(CB)[None, :]
    offdiag = jax.random.normal(key_off, (CENTRES, CB), jnp.float32) * (0.4 / math.sqrt(CB))
    diagonal = jax.random.uniform(key_diag, (CENTRES, 1), jnp.float32, 1.0, 2.0)
    return jnp.where(cols < rows, offdiag, 0.0) + jnp.where(cols == rows, diagonal, 0.0)


def shard_levels(own_key, extent, shards, low, top_value):
    def one(axis_at, parts):
        steps = jax.random.uniform(jax.random.fold_in(jax.random.fold_in(own_key, 6), axis_at), (parts,), jnp.float32, low / len(shards), top_value / len(shards))
        return jnp.repeat(jnp.exp(steps), extent[axis_at] // parts).reshape((-1,) + (1,) * (len(extent) - axis_at - 1))

    gain = one(*shards[0])
    for cut in shards[1:]:
        gain = gain * one(*cut)
    return gain


def normal_values(own_key, extent, scale, bound, cuts=(), kind=jnp.bfloat16):
    result = scale * jax.random.normal(own_key, extent, jnp.float32)
    if cuts:
        result = result * shard_levels(own_key, extent, cuts, -0.22, 0.18)
    return jnp.clip(result, -bound, bound).astype(kind)


def setup_inputs(seed: int = 0) -> dict:
    seeds = jax.random.split(jax.random.key(seed), 7)
    return {
        "points": draw_points(jax.random.fold_in(seeds[6], 71), 0),
        "centres": draw_centres(jax.random.fold_in(seeds[6], 71), 0),
        "factor": draw_factor(jax.random.fold_in(seeds[6], 71), 0),
        "solution": normal_values(seeds[3], (CENTRES, OUTS), 0.5, 4.0, ((0, 512),), jnp.float32),
        "residual": normal_values(seeds[4], (CENTRES, OUTS), 1.0, 6.0, ((0, 512),), jnp.float32),
        "direction": normal_values(seeds[5], (CENTRES, OUTS), 1.0, 6.0, ((0, 512),), jnp.float32),
    }


GAMMA_SCALE = 0.8
RIDGE = 64.0

def round_bf(values):
    return lax.optimization_barrier(values.astype(jnp.bfloat16)).astype(jnp.float32)

def precondition(factor, resid):
    width = factor.shape[1]
    blocks = factor.reshape(-1, width, width)
    rhs = resid.reshape(blocks.shape[0], width, resid.shape[1])
    lower = lax.linalg.triangular_solve(blocks, rhs, left_side=True, lower=True)
    upper = lax.linalg.triangular_solve(blocks, lower, left_side=True, lower=True, transpose_a=True)
    return upper.reshape(resid.shape)

def reference(points, centres, factor, solution, residual, direction):
    gamma = GAMMA_SCALE / math.sqrt(DIM)
    pts = points.astype(jnp.float32)
    cen = centres.astype(jnp.float32)
    gap_p = DIM - lax.optimization_barrier(jnp.sum(pts * pts, axis=1))
    gap_c = DIM - lax.optimization_barrier(jnp.sum(cen * cen, axis=1))
    block = min(512, POINTS)
    pts_blocks = pts.reshape(-1, block, DIM)
    gap_blocks = gap_p.reshape(-1, block)

    def apply_matrix(vector):
        vec_b = round_bf(vector)

        def step(acc, xs):
            rows, gap = xs
            cross = jnp.dot(rows, cen.T, precision=lax.Precision.HIGHEST)
            tile = round_bf(jnp.exp(gamma * (2.0 * cross + gap[:, None] + gap_c[None, :])))
            point_vals = round_bf(jnp.dot(tile, vec_b, precision=lax.Precision.HIGHEST))
            return (acc + jnp.dot(tile.T, point_vals, precision=lax.Precision.HIGHEST), None)
        start = jnp.zeros((CENTRES, OUTS), jnp.float32)
        total, _ = lax.scan(step, start, (pts_blocks, gap_blocks))
        return total / POINTS + RIDGE * vector
    coeffs, resid, search = (solution, residual, direction)
    precond = precondition(factor, resid)
    rz_now = jnp.sum(resid * precond)
    for step_index in range(ITERS):
        image = apply_matrix(search)
        alpha = rz_now / jnp.sum(search * image)
        coeffs = coeffs + alpha * search
        resid = resid - alpha * image
        if step_index + 1 < ITERS:
            precond = precondition(factor, resid)
            rz_next = jnp.sum(resid * precond)
            search = precond + rz_next / rz_now * search
            rz_now = rz_next
    return (coeffs, resid)
```

```python
import math

import jax
import jax.numpy as jnp
from jax import lax
from jax.sharding import Mesh, PartitionSpec as P

ITERS = 2
GAMMA_SCALE = 0.8
RIDGE = 64.0
CORES = 2
ROWS = 16
BF = jnp.bfloat16
F32 = jnp.float32


def row_gaps(rows):
    wide = rows.astype(F32)
    return rows.shape[1] - jnp.sum(wide * wide, axis=1)


def precondition(factor, resid):
    lower = lax.linalg.triangular_solve(factor, resid, left_side=True, lower=True)
    return lax.linalg.triangular_solve(factor, lower, left_side=True, lower=True, transpose_a=True)


def exchange(blocks, axes):
    return lax.all_to_all(blocks, axes, 0, 0, tiled=True)


def spread(block, axes):
    count = lax.axis_size(axes)
    return exchange(jnp.broadcast_to(block[None], (count,) + block.shape), axes)


def pack(scalars):
    values = jnp.stack(scalars)
    pieces = []
    for _ in range(3):
        piece = lax.reduce_precision(values, 8, 7)
        pieces.append(piece)
        values = values - piece
    flat = jnp.concatenate(pieces).astype(BF)
    return jnp.zeros((ROWS, 128), BF).at[0, : flat.shape[0]].set(flat)


def unpack(rows, count):
    wide = rows[:, 0, : 3 * count].astype(F32)
    return jnp.sum(wide.reshape(-1, 3, count), axis=(0, 1))


def body(points, centres, factor, solution, residual, direction):
    dim = points.shape[1]
    gamma = GAMMA_SCALE / math.sqrt(dim)
    outs = direction.shape[1]
    n_z, n_ctr = lax.axis_size("z"), lax.axis_size("ctr")
    n_a = CORES * n_ctr
    total_points = points.shape[0] * n_z * CORES
    share = points.shape[0] // n_ctr

    mine = lax.dynamic_slice_in_dim(points, lax.axis_index("ctr") * share, share, 0)
    pts = spread(mine, "z").reshape(n_z * share, dim)

    p0 = direction.T
    got = spread(jnp.concatenate([centres, p0.astype(BF)], 0), "ctr")
    got = lax.all_gather(got, "core", axis=0, tiled=True)
    cen = got[:, :dim].reshape(-1, dim)
    p0_all = got[:, dim:]

    gap_p, gap_c = row_gaps(pts), row_gaps(cen)
    cross = lax.dot_general(pts, cen, (((1,), (1,)), ((), ())), preferred_element_type=F32)
    tile = jnp.exp(gamma * (2.0 * cross + gap_p[:, None] + gap_c[None, :])).astype(BF)

    def apply(v_all, scalars):
        v = v_all.transpose(1, 0, 2).reshape(outs, -1)
        u = lax.dot_general(v, tile, (((1,), (1,)), ((), ())), preferred_element_type=F32)
        u = u.reshape(outs, -1, 128).transpose(1, 0, 2).reshape(n_z, -1, 128)
        u = jnp.sum(exchange(u, "z"), axis=0).astype(BF)
        u = spread(jnp.concatenate([u, pack(scalars)], 0), "z")
        local = unpack(u[:, -ROWS:], len(scalars))
        u = u[:, :-ROWS].reshape(-1, outs, 128).transpose(1, 0, 2).reshape(outs, -1)
        return u, local

    def back(u, scalars):
        v = jnp.dot(u, tile, preferred_element_type=F32)
        v = v.reshape(outs, n_a, 128).transpose(1, 0, 2)
        ride = jnp.zeros((8, 128), F32).at[0, : len(scalars)].set(jnp.stack(scalars))
        ride = jnp.broadcast_to(ride[None], (n_a, 8, 128))
        v = jnp.sum(exchange(jnp.concatenate([v, ride], 1), ("core", "ctr")), axis=0)
        return v[:-8] / total_points, v[-8, : len(scalars)]

    def dots(left, right):
        return jnp.sum(left.astype(F32) * right.astype(F32))

    def total(value):
        block = jnp.full((8, 128), value, F32)
        for axes in ("z", ("core", "ctr")):
            block = jnp.sum(spread(block, axes), axis=0)
        return block[0, 0]

    z0 = precondition(factor, residual)
    u0, s = apply(p0_all, [jnp.sum(residual * z0), dots(p0, p0)])
    v0, s = back(u0, [s[0], s[1], dots(u0, u0)])
    rz0 = s[0]
    q0 = v0 + RIDGE * p0
    alpha0 = rz0 / (s[2] / total_points + RIDGE * s[1])
    r1 = residual.T - alpha0 * q0
    z1 = precondition(factor, r1.T).T
    rz1 = total(dots(r1, z1))
    p1 = z1 + rz1 / rz0 * p0

    p1_all = spread(p1.astype(BF), "ctr")
    p1_all = lax.all_gather(p1_all, "core", axis=0, tiled=True)
    u1, s = apply(p1_all, [dots(p1, p1)])
    v1, s = back(u1, [s[0], dots(u1, u1)])
    q1 = v1 + RIDGE * p1
    alpha1 = rz1 / (s[1] / total_points + RIDGE * s[0])
    x2 = solution + (alpha0 * p0 + alpha1 * p1).T
    r2 = (r1 - alpha1 * q1).T
    return x2, r2


def solution(mesh):
    shape = (mesh.shape["pt"] // CORES, CORES, mesh.shape["ctr"])
    fine = Mesh(mesh.devices.reshape(shape), ("z", "core", "ctr"))
    rows = P(("z", "core", "ctr"), None)
    return jax.shard_map(
        body,
        mesh=fine,
        in_specs=(P(("z", "core"), None),) + (rows,) * 5,
        out_specs=(rows, rows),
        check_vma=False,
    )
```

```python
import functools
import math

import jax
import jax.numpy as jnp
from jax import lax
from jax.experimental import pallas as pl
from jax.experimental.pallas import tpu as pltpu
from jax.sharding import Mesh, PartitionSpec as P

GAMMA_SCALE = 0.8
RIDGE = 64.0
CORES = 2
LANES = 128
GROUP = 2
ROWS = 16
RIDE = 8
BF = jnp.bfloat16
F32 = jnp.float32
PARAMS = pltpu.CompilerParams(vmem_limit_bytes=40 * 1024 * 1024)


def row_gaps(rows):
    wide = rows.astype(F32)
    return rows.shape[1] - jnp.sum(wide * wide, axis=1)


def precondition(factor, resid):
    lower = lax.linalg.triangular_solve(factor, resid, left_side=True, lower=True)
    return lax.linalg.triangular_solve(factor, lower, left_side=True, lower=True, transpose_a=True)


def exchange(blocks, axes):
    return lax.all_to_all(blocks, axes, 0, 0, tiled=True)


def spread(block, axes):
    count = lax.axis_size(axes)
    return exchange(jnp.broadcast_to(block[None], (count,) + block.shape), axes)


def other_core(block):
    return lax.ppermute(block, "core", [(0, 1), (1, 0)])


def pack(rows):
    pieces = []
    for row in rows:
        for _ in range(3):
            piece = lax.reduce_precision(row, 8, 7)
            pieces.append(piece)
            row = row - piece
    pieces += [jnp.zeros_like(pieces[0])] * (ROWS - len(pieces))
    return jnp.stack(pieces).astype(BF)


def chunks_of(total):
    half = total.shape[0] // 2
    return [
        total[part * half : (part + 1) * half, at : at + LANES]
        for at in range(0, total.shape[1], LANES)
        for part in range(2)
    ]


def add_up(step, part, before_ref, u_ref, acc):
    @pl.when(step == 0)
    def _():
        acc[...] = part

    @pl.when(step > 0)
    def _():
        acc[...] += part

    @pl.when(step == pl.num_programs(0) - 1)
    def _():
        for at, piece in enumerate(chunks_of(acc[...])):
            u_ref[at] = piece if before_ref is None else piece + before_ref[at]


def build_kernel(gamma, first, pts_ref, gap_ref, blk_ref, *rest):
    before_ref = None if first else rest[0]
    tile_ref, u_ref, acc = rest[-3:]
    dim = pts_ref.shape[1]
    blk = blk_ref[...]
    cen = jnp.concatenate([blk[g, :LANES] for g in range(GROUP)], axis=0)
    vec = jnp.concatenate([blk[g, LANES:] for g in range(GROUP)], axis=1)
    wide = cen.astype(F32)
    gap_c = dim - jnp.sum(wide * wide, axis=1, keepdims=True)
    cross = lax.dot_general(cen, pts_ref[...], (((1,), (1,)), ((), ())), preferred_element_type=F32)
    tile = jnp.exp(gamma * (2.0 * cross + gap_c + gap_ref[...])).astype(BF)
    tile_ref[...] = tile
    part = jnp.dot(vec, tile, preferred_element_type=F32)
    add_up(pl.program_id(0), part, before_ref, u_ref, acc)


def apply_kernel(first, blk_ref, tile_ref, *rest):
    before_ref = None if first else rest[0]
    u_ref, acc = rest[-2:]
    blk = blk_ref[...]
    vec = jnp.concatenate([blk[g] for g in range(GROUP)], axis=1)
    part = jnp.dot(vec, tile_ref[...], preferred_element_type=F32)
    add_up(pl.program_id(0), part, before_ref, u_ref, acc)


def back_kernel(count, u_ref, tile_ref, v_ref, ub, ride):
    outs = ub.shape[0]
    half = outs // 2

    @pl.when(pl.program_id(0) == 0)
    def _():
        squares = jnp.zeros((half, LANES), F32)
        for at in range(u_ref.shape[0]):
            piece = u_ref[at, :half]
            low = (at % 2) * half
            ub[low : low + half, (at // 2) * LANES : (at // 2 + 1) * LANES] = piece
            squares += piece.astype(F32) * piece.astype(F32)
        packed = jnp.sum(u_ref[:, half:].astype(F32), axis=0)
        rows = [packed[3 * k : 3 * k + 1] + packed[3 * k + 1 : 3 * k + 2] + packed[3 * k + 2 : 3 * k + 3] for k in range(count)]
        rows.append(jnp.sum(squares, axis=0, keepdims=True))
        rows.append(jnp.zeros((RIDE - count - 1, LANES), F32))
        ride[...] = jnp.concatenate(rows, axis=0)

    v = lax.dot_general(ub[...], tile_ref[...], (((1,), (1,)), ((), ())), preferred_element_type=F32)
    for g in range(GROUP):
        v_ref[g, :outs] = v[:, g * LANES : (g + 1) * LANES]
        v_ref[g, outs:] = ride[...]


def body(points, centres, factor, solution, residual, direction):
    dim = points.shape[1]
    gamma = GAMMA_SCALE / math.sqrt(dim)
    outs = direction.shape[1]
    n_z, n_ctr = lax.axis_size("z"), lax.axis_size("ctr")
    total_points = points.shape[0] * n_z * CORES
    n_pts = points.shape[0]
    share = n_pts // n_ctr
    wide = GROUP * LANES
    grid = (n_ctr // GROUP,)
    u_shape = jax.ShapeDtypeStruct((2 * n_pts // LANES, outs // 2, LANES), F32)
    whole = lambda shape: pl.BlockSpec(shape, lambda i: (0,) * len(shape))
    blocks = lambda rows: pl.BlockSpec((GROUP, rows, LANES), lambda i: (i, 0, 0))
    tiles = pl.BlockSpec((wide, n_pts), lambda i: (i, 0))
    acc = pltpu.VMEM((outs, n_pts), F32)
    work = n_ctr * LANES * n_pts

    def cost(flops, exps, size):
        return pl.CostEstimate(flops=flops, transcendentals=exps, bytes_accessed=size)

    def build(pts, gap, blk, before):
        first = before is None
        extra = [] if first else [before]
        return pl.pallas_call(
            functools.partial(build_kernel, gamma, first),
            grid=grid,
            in_specs=[whole(pts.shape), whole(gap.shape), blocks(blk.shape[1])] + [whole(u_shape.shape)] * len(extra),
            out_specs=[tiles, whole(u_shape.shape)],
            out_shape=[jax.ShapeDtypeStruct((n_ctr * LANES, n_pts), BF), u_shape],
            scratch_shapes=[acc],
            compiler_params=PARAMS,
            cost_estimate=cost(2 * work * (dim + outs), work, 2 * work),
            name="build_tile",
        )(pts, gap, blk, *extra)

    def apply(blk, tile, before):
        first = before is None
        extra = [] if first else [before]
        return pl.pallas_call(
            functools.partial(apply_kernel, first),
            grid=grid,
            in_specs=[blocks(outs), tiles] + [whole(u_shape.shape)] * len(extra),
            out_specs=whole(u_shape.shape),
            out_shape=u_shape,
            scratch_shapes=[acc],
            compiler_params=PARAMS,
            cost_estimate=cost(2 * work * outs, 0, 2 * work),
            name="apply_tile",
        )(blk, tile, *extra)

    def back(u, tile, count):
        return pl.pallas_call(
            functools.partial(back_kernel, count),
            grid=grid,
            in_specs=[whole(u.shape), tiles],
            out_specs=blocks(outs + RIDE),
            out_shape=jax.ShapeDtypeStruct((n_ctr, outs + RIDE, LANES), F32),
            scratch_shapes=[pltpu.VMEM((outs, n_pts), BF), pltpu.VMEM((RIDE, LANES), F32)],
            compiler_params=PARAMS,
            cost_estimate=cost(2 * work * outs, 0, 2 * work),
            name="back_tile",
        )(u, tile)

    def reduce_points(u, rows):
        u = jnp.sum(exchange(u, "z"), axis=0).astype(BF)
        return spread(jnp.concatenate([u, pack(rows)], 0), "z")

    def reduce_centres(u, tile, tile_other, count):
        v = other_core(back(u, tile_other, count))
        v = back(u, tile, count) + v
        v = jnp.sum(exchange(v, "ctr"), axis=0)
        return v[:outs] / total_points, jnp.sum(v[outs : outs + count + 1], axis=1)

    def lanes(left, right):
        return jnp.sum(left * right, axis=0)

    mine = lax.dynamic_slice_in_dim(points, lax.axis_index("ctr") * share, share, 0)
    pts = spread(mine, "z").reshape(n_pts, dim)
    gap = row_gaps(pts)[None]
    p0 = direction.T
    own = spread(jnp.concatenate([centres, p0.astype(BF)], 0), "ctr")
    other = other_core(own)

    tile, u0 = build(pts, gap, own, None)
    tile_other, u0 = build(pts, gap, other, u0)
    z0 = precondition(factor, residual)
    u0 = reduce_points(u0, [lanes(residual.T, z0.T), lanes(p0, p0)])
    v0, s = reduce_centres(u0, tile, tile_other, 2)
    rz0 = s[0]
    q0 = v0 + RIDGE * p0
    alpha0 = rz0 / (s[2] / total_points + RIDGE * s[1])
    r1 = residual.T - alpha0 * q0
    z1 = precondition(factor, r1.T).T
    block = jnp.broadcast_to(lanes(r1, z1)[None], (RIDE, LANES))
    for axes in ("z", ("core", "ctr")):
        block = jnp.sum(spread(block, axes), axis=0)
    rz1 = jnp.sum(block[0])
    p1 = z1 + rz1 / rz0 * p0

    own = spread(p1.astype(BF), "ctr")
    other = other_core(own)
    u1 = apply(own, tile, None)
    u1 = apply(other, tile_other, u1)
    u1 = reduce_points(u1, [lanes(p1, p1)])
    v1, s = reduce_centres(u1, tile, tile_other, 1)
    q1 = v1 + RIDGE * p1
    alpha1 = rz1 / (s[1] / total_points + RIDGE * s[0])
    x2 = solution + (alpha0 * p0 + alpha1 * p1).T
    r2 = (r1 - alpha1 * q1).T
    return x2, r2


def solution(mesh):
    shape = (mesh.shape["pt"] // CORES, CORES, mesh.shape["ctr"])
    fine = Mesh(mesh.devices.reshape(shape), ("z", "core", "ctr"))
    rows = P(("z", "core", "ctr"), None)
    return jax.shard_map(
        body,
        mesh=fine,
        in_specs=(P(("z", "core"), None),) + (rows,) * 5,
        out_specs=(rows, rows),
        check_vma=False,
    )
```

```python
import functools
import math

import jax
import jax.numpy as jnp
from jax import lax
from jax.experimental import pallas as pl
from jax.experimental.pallas import tpu as pltpu
from jax.sharding import Mesh, PartitionSpec as P

GAMMA_SCALE = 0.8
RIDGE = 64.0
CORES = 2
LANES = 128
GROUP = 2
ROWS = 16
RIDE = 8
BF = jnp.bfloat16
F32 = jnp.float32
PARAMS = pltpu.CompilerParams(vmem_limit_bytes=60 * 1024 * 1024)


def row_gaps(rows):
    wide = rows.astype(F32)
    return rows.shape[1] - jnp.sum(wide * wide, axis=1)


def precondition(factor, resid):
    lower = lax.linalg.triangular_solve(factor, resid, left_side=True, lower=True)
    return lax.linalg.triangular_solve(factor, lower, left_side=True, lower=True, transpose_a=True)


def exchange(blocks, axes):
    return lax.all_to_all(blocks, axes, 0, 0, tiled=True)


def spread(block, axes):
    count = lax.axis_size(axes)
    return exchange(jnp.broadcast_to(block[None], (count,) + block.shape), axes)


def other_core(block):
    return lax.ppermute(block, "core", [(0, 1), (1, 0)])


def pack(rows):
    pieces = []
    for row in rows:
        for _ in range(3):
            piece = lax.reduce_precision(row, 8, 7)
            pieces.append(piece)
            row = row - piece
    pieces += [jnp.zeros_like(pieces[0])] * (ROWS - len(pieces))
    return jnp.stack(pieces).astype(BF)


def chunks_of(total):
    half = total.shape[0] // 2
    return [
        total[part * half : (part + 1) * half, at : at + LANES]
        for at in range(0, total.shape[1], LANES)
        for part in range(2)
    ]


def add_up(step, part, before_ref, u_ref, acc):
    @pl.when(step == 0)
    def _():
        acc[...] = part

    @pl.when(step > 0)
    def _():
        acc[...] += part

    @pl.when(step == pl.num_programs(0) - 1)
    def _():
        for at, piece in enumerate(chunks_of(acc[...])):
            u_ref[at] = piece if before_ref is None else piece + before_ref[at]


def build_kernel(gamma, first, pts_ref, gap_ref, blk_ref, *rest):
    before_ref = None if first else rest[0]
    tile_ref, u_ref, acc = rest[-3:]
    dim = pts_ref.shape[1]
    blk = blk_ref[...]
    cen = jnp.concatenate([blk[g, :LANES] for g in range(GROUP)], axis=0)
    vec = jnp.concatenate([blk[g, LANES:] for g in range(GROUP)], axis=1)
    wide = cen.astype(F32)
    gap_c = dim - jnp.sum(wide * wide, axis=1, keepdims=True)
    cross = lax.dot_general(cen, pts_ref[...], (((1,), (1,)), ((), ())), preferred_element_type=F32)
    tile = jnp.exp(gamma * (2.0 * cross + gap_c + gap_ref[...])).astype(BF)
    tile_ref[...] = tile
    part = jnp.dot(vec, tile, preferred_element_type=F32)
    add_up(pl.program_id(0), part, before_ref, u_ref, acc)


def apply_kernel(first, blk_ref, tile_ref, *rest):
    before_ref = None if first else rest[0]
    u_ref, acc = rest[-2:]
    blk = blk_ref[...]
    vec = jnp.concatenate([blk[g] for g in range(GROUP)], axis=1)
    part = jnp.dot(vec, tile_ref[...], preferred_element_type=F32)
    add_up(pl.program_id(0), part, before_ref, u_ref, acc)


def back_kernel(count, u_ref, tile_ref, v_ref, ub, ride):
    outs = ub.shape[0]
    half = outs // 2

    @pl.when(pl.program_id(0) == 0)
    def _():
        squares = jnp.zeros((half, LANES), F32)
        for at in range(u_ref.shape[0]):
            piece = u_ref[at, :half]
            low = (at % 2) * half
            ub[low : low + half, (at // 2) * LANES : (at // 2 + 1) * LANES] = piece
            squares += piece.astype(F32) * piece.astype(F32)
        packed = jnp.sum(u_ref[:, half:].astype(F32), axis=0) if count else None
        rows = [packed[3 * k : 3 * k + 1] + packed[3 * k + 1 : 3 * k + 2] + packed[3 * k + 2 : 3 * k + 3] for k in range(count)]
        rows.append(jnp.sum(squares, axis=0, keepdims=True))
        rows.append(jnp.zeros((RIDE - count - 1, LANES), F32))
        ride[...] = jnp.concatenate(rows, axis=0)

    v = lax.dot_general(ub[...], tile_ref[...], (((1,), (1,)), ((), ())), preferred_element_type=F32)
    for g in range(GROUP):
        v_ref[g, :outs] = v[:, g * LANES : (g + 1) * LANES]
        v_ref[g, outs:] = ride[...]


def body(points, centres, factor, solution, residual, direction):
    dim = points.shape[1]
    gamma = GAMMA_SCALE / math.sqrt(dim)
    outs = direction.shape[1]
    n_z, n_ctr = lax.axis_size("z"), lax.axis_size("ctr")
    total_points = points.shape[0] * n_z * CORES
    n_pts = points.shape[0]
    share = n_pts // n_ctr
    wide = GROUP * LANES
    grid = (n_ctr // GROUP,)
    u_shape = jax.ShapeDtypeStruct((2 * n_pts // LANES, outs // 2, LANES), F32)
    whole = lambda shape: pl.BlockSpec(shape, lambda i: (0,) * len(shape))
    blocks = lambda rows: pl.BlockSpec((GROUP, rows, LANES), lambda i: (i, 0, 0))
    tiles = pl.BlockSpec((wide, n_pts), lambda i: (i, 0))
    acc = pltpu.VMEM((outs, n_pts), F32)
    work = n_ctr * LANES * n_pts

    def cost(flops, exps, size):
        return pl.CostEstimate(flops=flops, transcendentals=exps, bytes_accessed=size)

    def build(pts, gap, blk, before):
        first = before is None
        extra = [] if first else [before]
        return pl.pallas_call(
            functools.partial(build_kernel, gamma, first),
            grid=grid,
            in_specs=[whole(pts.shape), whole(gap.shape), blocks(blk.shape[1])] + [whole(u_shape.shape)] * len(extra),
            out_specs=[tiles, whole(u_shape.shape)],
            out_shape=[jax.ShapeDtypeStruct((n_ctr * LANES, n_pts), BF), u_shape],
            scratch_shapes=[acc],
            compiler_params=PARAMS,
            cost_estimate=cost(2 * work * (dim + outs), work, 2 * work),
            name="build_tile",
        )(pts, gap, blk, *extra)

    def apply(blk, tile, before):
        first = before is None
        extra = [] if first else [before]
        return pl.pallas_call(
            functools.partial(apply_kernel, first),
            grid=grid,
            in_specs=[blocks(outs), tiles] + [whole(u_shape.shape)] * len(extra),
            out_specs=whole(u_shape.shape),
            out_shape=u_shape,
            scratch_shapes=[acc],
            compiler_params=PARAMS,
            cost_estimate=cost(2 * work * outs, 0, 2 * work),
            name="apply_tile",
        )(blk, tile, *extra)

    def back(u, tile, count):
        return pl.pallas_call(
            functools.partial(back_kernel, count),
            grid=grid,
            in_specs=[whole(u.shape), tiles],
            out_specs=blocks(outs + RIDE),
            out_shape=jax.ShapeDtypeStruct((n_ctr, outs + RIDE, LANES), F32),
            scratch_shapes=[pltpu.VMEM((outs, n_pts), BF), pltpu.VMEM((RIDE, LANES), F32)],
            compiler_params=PARAMS,
            cost_estimate=cost(2 * work * outs, 0, 2 * work),
            name="back_tile",
        )(u, tile)

    def reduce_points(u, rows):
        u = jnp.sum(exchange(u, "z"), axis=0).astype(BF)
        return spread(jnp.concatenate([u, pack(rows)], 0) if rows else u, "z")

    def reduce_centres(u, tile, tile_other, count):
        v = other_core(back(u, tile_other, count))
        v = back(u, tile, count) + v
        v = jnp.sum(exchange(v, "ctr"), axis=0)
        return v[:outs] / total_points, jnp.sum(v[outs : outs + count + 1], axis=1)

    def lanes(left, right):
        return jnp.sum(left * right, axis=0)

    mine = lax.dynamic_slice_in_dim(points, lax.axis_index("ctr") * share, share, 0)
    pts = spread(mine, "z").reshape(n_pts, dim)
    gap = row_gaps(pts)[None]
    p0 = direction.T
    own = spread(jnp.concatenate([centres, p0.astype(BF)], 0), "ctr")
    other = other_core(own)

    tile, u0 = build(pts, gap, own, None)
    tile_other, u0 = build(pts, gap, other, u0)
    z0 = precondition(factor, residual)
    u0 = reduce_points(u0, [lanes(residual.T, z0.T), lanes(p0, p0)])
    v0, s = reduce_centres(u0, tile, tile_other, 2)
    rz0 = s[0]
    q0 = v0 + RIDGE * p0
    alpha0 = rz0 / (s[2] / total_points + RIDGE * s[1])
    r1 = residual.T - alpha0 * q0
    z1 = precondition(factor, r1.T).T
    block = jnp.stack([lanes(r1, z1), lanes(z1, z1), lanes(z1, p0)] + [jnp.zeros((LANES,), F32)] * (RIDE - 3))
    for axes in ("z", ("core", "ctr")):
        block = jnp.sum(spread(block, axes), axis=0)
    rz1, zz, zp = [jnp.sum(block[k]) for k in range(3)]
    beta = rz1 / rz0
    p1 = z1 + beta * p0
    pp = zz + beta * (2.0 * zp + beta * s[1])

    own = spread(p1.astype(BF), "ctr")
    other = other_core(own)
    u1 = apply(own, tile, None)
    u1 = apply(other, tile_other, u1)
    u1 = reduce_points(u1, [])
    v1, s = reduce_centres(u1, tile, tile_other, 0)
    q1 = v1 + RIDGE * p1
    alpha1 = rz1 / (s[0] / total_points + RIDGE * pp)
    x2 = solution + (alpha0 * p0 + alpha1 * p1).T
    r2 = (r1 - alpha1 * q1).T
    return x2, r2


def solution(mesh):
    shape = (mesh.shape["pt"] // CORES, CORES, mesh.shape["ctr"])
    fine = Mesh(mesh.devices.reshape(shape), ("z", "core", "ctr"))
    rows = P(("z", "core", "ctr"), None)
    return jax.shard_map(
        body,
        mesh=fine,
        in_specs=(P(("z", "core"), None),) + (rows,) * 5,
        out_specs=(rows, rows),
        check_vma=False,
    )
```

```python
import functools
import math

import jax
import jax.numpy as jnp
from jax import lax
from jax.experimental import pallas as pl
from jax.experimental.pallas import tpu as pltpu
from jax.sharding import Mesh, PartitionSpec as P

GAMMA_SCALE = 0.8
RIDGE = 64.0
CORES = 2
LANES = 128
GROUP = 2
ROWS = 16
RIDE = 8
BF = jnp.bfloat16
F32 = jnp.float32
PARAMS = pltpu.CompilerParams(vmem_limit_bytes=16 * 1024 * 1024)


def row_gaps(rows):
    wide = rows.astype(F32)
    return rows.shape[1] - jnp.sum(wide * wide, axis=1)


def precondition(factor, resid):
    lower = lax.linalg.triangular_solve(factor, resid, left_side=True, lower=True)
    return lax.linalg.triangular_solve(factor, lower, left_side=True, lower=True, transpose_a=True)


def exchange(blocks, axes):
    return lax.all_to_all(blocks, axes, 0, 0, tiled=True)


def spread(block, axes):
    count = lax.axis_size(axes)
    return exchange(jnp.broadcast_to(block[None], (count,) + block.shape), axes)


def other_core(block):
    return lax.ppermute(block, "core", [(0, 1), (1, 0)])


def pack(rows):
    pieces = []
    for row in rows:
        for _ in range(3):
            piece = lax.reduce_precision(row, 8, 7)
            pieces.append(piece)
            row = row - piece
    pieces += [jnp.zeros_like(pieces[0])] * (ROWS - len(pieces))
    return jnp.stack(pieces).astype(BF)


def chunks_of(total):
    half = total.shape[0] // 2
    return [
        total[part * half : (part + 1) * half, at : at + LANES]
        for at in range(0, total.shape[1], LANES)
        for part in range(2)
    ]


def add_up(step, part, before_ref, u_ref, acc):
    @pl.when(step == 0)
    def _():
        acc[...] = part

    @pl.when(step > 0)
    def _():
        acc[...] += part

    @pl.when(step == pl.num_programs(0) - 1)
    def _():
        for at, piece in enumerate(chunks_of(acc[...])):
            u_ref[at] = piece if before_ref is None else piece + before_ref[at]


def build_kernel(gamma, first, pts_ref, gap_ref, blk_ref, *rest):
    before_ref = None if first else rest[0]
    tile_ref, u_ref, acc = rest[-3:]
    dim = pts_ref.shape[1]
    blk = blk_ref[...]
    cen = jnp.concatenate([blk[g, :LANES] for g in range(GROUP)], axis=0)
    vec = jnp.concatenate([blk[g, LANES:] for g in range(GROUP)], axis=1)
    wide = cen.astype(F32)
    gap_c = dim - jnp.sum(wide * wide, axis=1, keepdims=True)
    cross = lax.dot_general(cen, pts_ref[...], (((1,), (1,)), ((), ())), preferred_element_type=F32)
    tile = jnp.exp(gamma * (2.0 * cross + gap_c + gap_ref[...])).astype(BF)
    tile_ref[...] = tile
    part = jnp.dot(vec, tile, preferred_element_type=F32)
    add_up(pl.program_id(0), part, before_ref, u_ref, acc)


def apply_kernel(first, blk_ref, tile_ref, *rest):
    before_ref = None if first else rest[0]
    u_ref, acc = rest[-2:]
    blk = blk_ref[...]
    vec = jnp.concatenate([blk[g] for g in range(GROUP)], axis=1)
    part = jnp.dot(vec, tile_ref[...], preferred_element_type=F32)
    add_up(pl.program_id(0), part, before_ref, u_ref, acc)


def back_kernel(count, u_ref, tile_ref, v_ref, ub, ride):
    outs = ub.shape[0]
    half = outs // 2

    @pl.when(pl.program_id(0) == 0)
    def _():
        squares = jnp.zeros((half, LANES), F32)
        for at in range(u_ref.shape[0]):
            piece = u_ref[at, :half]
            low = (at % 2) * half
            ub[low : low + half, (at // 2) * LANES : (at // 2 + 1) * LANES] = piece
            squares += piece.astype(F32) * piece.astype(F32)
        packed = jnp.sum(u_ref[:, half:].astype(F32), axis=0) if count else None
        rows = [packed[3 * k : 3 * k + 1] + packed[3 * k + 1 : 3 * k + 2] + packed[3 * k + 2 : 3 * k + 3] for k in range(count)]
        rows.append(jnp.sum(squares, axis=0, keepdims=True))
        rows.append(jnp.zeros((RIDE - count - 1, LANES), F32))
        ride[...] = jnp.concatenate(rows, axis=0)

    v = lax.dot_general(ub[...], tile_ref[...], (((1,), (1,)), ((), ())), preferred_element_type=F32)
    for g in range(GROUP):
        v_ref[g, :outs] = v[:, g * LANES : (g + 1) * LANES]
        v_ref[g, outs:] = ride[...]


def body(points, centres, factor, solution, residual, direction):
    dim = points.shape[1]
    gamma = GAMMA_SCALE / math.sqrt(dim)
    outs = direction.shape[1]
    n_z, n_ctr = lax.axis_size("z"), lax.axis_size("ctr")
    total_points = points.shape[0] * n_z * CORES
    n_pts = points.shape[0]
    share = n_pts // n_ctr
    wide = GROUP * LANES
    grid = (n_ctr // GROUP,)
    u_shape = jax.ShapeDtypeStruct((2 * n_pts // LANES, outs // 2, LANES), F32)
    whole = lambda shape: pl.BlockSpec(shape, lambda i: (0,) * len(shape))
    blocks = lambda rows: pl.BlockSpec((GROUP, rows, LANES), lambda i: (i, 0, 0))
    tiles = pl.BlockSpec((wide, n_pts), lambda i: (i, 0))
    acc = pltpu.VMEM((outs, n_pts), F32)
    work = n_ctr * LANES * n_pts

    def cost(flops, exps, size):
        return pl.CostEstimate(flops=flops, transcendentals=exps, bytes_accessed=size)

    def build(pts, gap, blk, before):
        first = before is None
        extra = [] if first else [before]
        return pl.pallas_call(
            functools.partial(build_kernel, gamma, first),
            grid=grid,
            in_specs=[whole(pts.shape), whole(gap.shape), blocks(blk.shape[1])] + [whole(u_shape.shape)] * len(extra),
            out_specs=[tiles, whole(u_shape.shape)],
            out_shape=[jax.ShapeDtypeStruct((n_ctr * LANES, n_pts), BF), u_shape],
            scratch_shapes=[acc],
            compiler_params=PARAMS,
            cost_estimate=cost(2 * work * (dim + outs), work, 2 * work),
            name="build_tile",
        )(pts, gap, blk, *extra)

    def apply(blk, tile, before):
        first = before is None
        extra = [] if first else [before]
        return pl.pallas_call(
            functools.partial(apply_kernel, first),
            grid=grid,
            in_specs=[blocks(outs), tiles] + [whole(u_shape.shape)] * len(extra),
            out_specs=whole(u_shape.shape),
            out_shape=u_shape,
            scratch_shapes=[acc],
            compiler_params=PARAMS,
            cost_estimate=cost(2 * work * outs, 0, 2 * work),
            name="apply_tile",
        )(blk, tile, *extra)

    def back(u, tile, count):
        return pl.pallas_call(
            functools.partial(back_kernel, count),
            grid=grid,
            in_specs=[whole(u.shape), tiles],
            out_specs=blocks(outs + RIDE),
            out_shape=jax.ShapeDtypeStruct((n_ctr, outs + RIDE, LANES), F32),
            scratch_shapes=[pltpu.VMEM((outs, n_pts), BF), pltpu.VMEM((RIDE, LANES), F32)],
            compiler_params=PARAMS,
            cost_estimate=cost(2 * work * outs, 0, 2 * work),
            name="back_tile",
        )(u, tile)

    def reduce_points(u, rows):
        u = jnp.sum(exchange(u, "z"), axis=0).astype(BF)
        return spread(jnp.concatenate([u, pack(rows)], 0) if rows else u, "z")

    def reduce_centres(u, tile, tile_other, count):
        v = other_core(back(u, tile_other, count))
        v = back(u, tile, count) + v
        v = jnp.sum(exchange(v, "ctr"), axis=0)
        return v[:outs] / total_points, jnp.sum(v[outs : outs + count + 1], axis=1)

    def lanes(left, right):
        return jnp.sum(left * right, axis=0)

    mine = lax.dynamic_slice_in_dim(points, lax.axis_index("ctr") * share, share, 0)
    pts = spread(mine, "z").reshape(n_pts, dim)
    gap = row_gaps(pts)[None]
    p0 = direction.T
    own = spread(jnp.concatenate([centres, p0.astype(BF)], 0), "ctr")
    other = other_core(own)

    tile, u0 = build(pts, gap, own, None)
    tile_other, u0 = build(pts, gap, other, u0)
    z0 = precondition(factor, residual)
    u0 = reduce_points(u0, [lanes(residual.T, z0.T), lanes(p0, p0)])
    v0, s = reduce_centres(u0, tile, tile_other, 2)
    rz0 = s[0]
    q0 = v0 + RIDGE * p0
    alpha0 = rz0 / (s[2] / total_points + RIDGE * s[1])
    r1 = residual.T - alpha0 * q0
    z1 = precondition(factor, r1.T).T
    block = jnp.stack([lanes(r1, z1), lanes(z1, z1), lanes(z1, p0)] + [jnp.zeros((LANES,), F32)] * (RIDE - 3))
    for axes in ("z", ("core", "ctr")):
        block = jnp.sum(spread(block, axes), axis=0)
    rz1, zz, zp = [jnp.sum(block[k]) for k in range(3)]
    beta = rz1 / rz0
    p1 = z1 + beta * p0
    pp = zz + beta * (2.0 * zp + beta * s[1])

    own = spread(p1.astype(BF), "ctr")
    other = other_core(own)
    u1 = apply(own, tile, None)
    u1 = apply(other, tile_other, u1)
    u1 = reduce_points(u1, [])
    v1, s = reduce_centres(u1, tile, tile_other, 0)
    q1 = v1 + RIDGE * p1
    alpha1 = rz1 / (s[0] / total_points + RIDGE * pp)
    x2 = solution + (alpha0 * p0 + alpha1 * p1).T
    r2 = (r1 - alpha1 * q1).T
    return x2, r2


def solution(mesh):
    shape = (mesh.shape["pt"] // CORES, CORES, mesh.shape["ctr"])
    fine = Mesh(mesh.devices.reshape(shape), ("z", "core", "ctr"))
    rows = P(("z", "core", "ctr"), None)
    return jax.shard_map(
        body,
        mesh=fine,
        in_specs=(P(("z", "core"), None),) + (rows,) * 5,
        out_specs=(rows, rows),
        check_vma=False,
    )
```

```python
import functools
import math

import jax
import jax.numpy as jnp
from jax import lax
from jax.experimental import pallas as pl
from jax.experimental.pallas import tpu as pltpu
from jax.sharding import Mesh, PartitionSpec as P

GAMMA_SCALE = 0.8
RIDGE = 64.0
CORES = 2
LANES = 128
GROUP = 2
ROWS = 16
RIDE = 8
BF = jnp.bfloat16
F32 = jnp.float32
PARAMS = pltpu.CompilerParams(vmem_limit_bytes=24 * 1024 * 1024)


def row_gaps(rows):
    wide = rows.astype(F32)
    return rows.shape[1] - jnp.sum(wide * wide, axis=1)


def precondition(factor, resid):
    lower = lax.linalg.triangular_solve(factor, resid, left_side=True, lower=True)
    return lax.linalg.triangular_solve(factor, lower, left_side=True, lower=True, transpose_a=True)


def exchange(blocks, axes):
    return lax.all_to_all(blocks, axes, 0, 0, tiled=True)


def spread(block, axes):
    count = lax.axis_size(axes)
    return exchange(jnp.broadcast_to(block[None], (count,) + block.shape), axes)


def other_core(block):
    return lax.ppermute(block, "core", [(0, 1), (1, 0)])


def pack(rows):
    pieces = []
    for row in rows:
        for _ in range(3):
            piece = lax.reduce_precision(row, 8, 7)
            pieces.append(piece)
            row = row - piece
    pieces += [jnp.zeros_like(pieces[0])] * (ROWS - len(pieces))
    return jnp.stack(pieces).astype(BF)


def chunks_of(total):
    half = total.shape[0] // 2
    return [
        total[part * half : (part + 1) * half, at : at + LANES]
        for at in range(0, total.shape[1], LANES)
        for part in range(2)
    ]


def add_up(step, part, before_ref, u_ref, acc):
    @pl.when(step == 0)
    def _():
        acc[...] = part

    @pl.when(step > 0)
    def _():
        acc[...] += part

    @pl.when(step == pl.num_programs(0) - 1)
    def _():
        for at, piece in enumerate(chunks_of(acc[...])):
            u_ref[at] = piece if before_ref is None else piece + before_ref[at]


def rows_at(step):
    rows = GROUP * LANES
    return pl.ds(pl.multiple_of(step * rows, rows), rows)


def tile_copy(source, target, sems, step):
    rows = rows_at(step)
    return pltpu.make_async_copy(source.at[rows], target.at[rows], sems.at[step])


def fetch(step, tile_ref, buf, sems):
    @pl.when(step == 0)
    def _():
        for at in range(sems.shape[0]):
            tile_copy(tile_ref, buf, sems, at).start()

    tile_copy(tile_ref, buf, sems, step).wait()
    return buf[rows_at(step)]


def build_kernel(gamma, first, pts_ref, gap_ref, blk_ref, *rest):
    before_ref = None if first else rest[0]
    tile_ref, u_ref, acc, buf, sems = rest[-5:]
    step = pl.program_id(0)
    dim = pts_ref.shape[1]
    blk = blk_ref[...]
    cen = jnp.concatenate([blk[g, :LANES] for g in range(GROUP)], axis=0)
    vec = jnp.concatenate([blk[g, LANES:] for g in range(GROUP)], axis=1)
    wide = cen.astype(F32)
    gap_c = dim - jnp.sum(wide * wide, axis=1, keepdims=True)
    cross = lax.dot_general(cen, pts_ref[...], (((1,), (1,)), ((), ())), preferred_element_type=F32)
    tile = jnp.exp(gamma * (2.0 * cross + gap_c + gap_ref[...])).astype(BF)
    buf[rows_at(step)] = tile
    tile_copy(buf, tile_ref, sems, step).start()
    part = jnp.dot(vec, tile, preferred_element_type=F32)
    add_up(step, part, before_ref, u_ref, acc)

    @pl.when(step == pl.num_programs(0) - 1)
    def _():
        for at in range(sems.shape[0]):
            tile_copy(buf, tile_ref, sems, at).wait()


def apply_kernel(first, blk_ref, tile_ref, *rest):
    before_ref = None if first else rest[0]
    u_ref, acc, buf, sems = rest[-4:]
    step = pl.program_id(0)
    tile = fetch(step, tile_ref, buf, sems)
    blk = blk_ref[...]
    vec = jnp.concatenate([blk[g] for g in range(GROUP)], axis=1)
    part = jnp.dot(vec, tile, preferred_element_type=F32)
    add_up(step, part, before_ref, u_ref, acc)


def back_kernel(count, u_ref, tile_ref, v_ref, ub, ride, buf, sems):
    outs = ub.shape[0]
    half = outs // 2
    step = pl.program_id(0)
    tile = fetch(step, tile_ref, buf, sems)

    @pl.when(step == 0)
    def _():
        squares = jnp.zeros((half, LANES), F32)
        for at in range(u_ref.shape[0]):
            piece = u_ref[at, :half]
            low = (at % 2) * half
            ub[low : low + half, (at // 2) * LANES : (at // 2 + 1) * LANES] = piece
            squares += piece.astype(F32) * piece.astype(F32)
        packed = jnp.sum(u_ref[:, half:].astype(F32), axis=0) if count else None
        rows = [packed[3 * k : 3 * k + 1] + packed[3 * k + 1 : 3 * k + 2] + packed[3 * k + 2 : 3 * k + 3] for k in range(count)]
        rows.append(jnp.sum(squares, axis=0, keepdims=True))
        rows.append(jnp.zeros((RIDE - count - 1, LANES), F32))
        ride[...] = jnp.concatenate(rows, axis=0)

    v = lax.dot_general(ub[...], tile, (((1,), (1,)), ((), ())), preferred_element_type=F32)
    for g in range(GROUP):
        v_ref[g, :outs] = v[:, g * LANES : (g + 1) * LANES]
        v_ref[g, outs:] = ride[...]


def body(points, centres, factor, solution, residual, direction):
    dim = points.shape[1]
    gamma = GAMMA_SCALE / math.sqrt(dim)
    outs = direction.shape[1]
    n_z, n_ctr = lax.axis_size("z"), lax.axis_size("ctr")
    total_points = points.shape[0] * n_z * CORES
    n_pts = points.shape[0]
    share = n_pts // n_ctr
    grid = (n_ctr // GROUP,)
    u_shape = jax.ShapeDtypeStruct((2 * n_pts // LANES, outs // 2, LANES), F32)
    whole = lambda shape: pl.BlockSpec(shape, lambda i: (0,) * len(shape))
    blocks = lambda rows: pl.BlockSpec((GROUP, rows, LANES), lambda i: (i, 0, 0))
    tiles = pl.BlockSpec(memory_space=pltpu.HBM)
    copies = [pltpu.VMEM((n_ctr * LANES, n_pts), BF), pltpu.SemaphoreType.DMA(grid)]
    acc = pltpu.VMEM((outs, n_pts), F32)
    work = n_ctr * LANES * n_pts

    def cost(flops, exps, size):
        return pl.CostEstimate(flops=flops, transcendentals=exps, bytes_accessed=size)

    def build(pts, gap, blk, before):
        first = before is None
        extra = [] if first else [before]
        return pl.pallas_call(
            functools.partial(build_kernel, gamma, first),
            grid=grid,
            in_specs=[whole(pts.shape), whole(gap.shape), blocks(blk.shape[1])] + [whole(u_shape.shape)] * len(extra),
            out_specs=[tiles, whole(u_shape.shape)],
            out_shape=[jax.ShapeDtypeStruct((n_ctr * LANES, n_pts), BF), u_shape],
            scratch_shapes=[acc] + copies,
            compiler_params=PARAMS,
            cost_estimate=cost(2 * work * (dim + outs), work, 2 * work),
            name="build_tile",
        )(pts, gap, blk, *extra)

    def apply(blk, tile, before):
        first = before is None
        extra = [] if first else [before]
        return pl.pallas_call(
            functools.partial(apply_kernel, first),
            grid=grid,
            in_specs=[blocks(outs), tiles] + [whole(u_shape.shape)] * len(extra),
            out_specs=whole(u_shape.shape),
            out_shape=u_shape,
            scratch_shapes=[acc] + copies,
            compiler_params=PARAMS,
            cost_estimate=cost(2 * work * outs, 0, 2 * work),
            name="apply_tile",
        )(blk, tile, *extra)

    def back(u, tile, count):
        return pl.pallas_call(
            functools.partial(back_kernel, count),
            grid=grid,
            in_specs=[whole(u.shape), tiles],
            out_specs=blocks(outs + RIDE),
            out_shape=jax.ShapeDtypeStruct((n_ctr, outs + RIDE, LANES), F32),
            scratch_shapes=[pltpu.VMEM((outs, n_pts), BF), pltpu.VMEM((RIDE, LANES), F32)] + copies,
            compiler_params=PARAMS,
            cost_estimate=cost(2 * work * outs, 0, 2 * work),
            name="back_tile",
        )(u, tile)

    def reduce_points(u, rows):
        u = jnp.sum(exchange(u, "z"), axis=0).astype(BF)
        return spread(jnp.concatenate([u, pack(rows)], 0) if rows else u, "z")

    def reduce_centres(u, tile, tile_other, count):
        v = other_core(back(u, tile_other, count))
        v = back(u, tile, count) + v
        v = jnp.sum(exchange(v, "ctr"), axis=0)
        return v[:outs] / total_points, jnp.sum(v[outs : outs + count + 1], axis=1)

    def lanes(left, right):
        return jnp.sum(left * right, axis=0)

    mine = lax.dynamic_slice_in_dim(points, lax.axis_index("ctr") * share, share, 0)
    pts = spread(mine, "z").reshape(n_pts, dim)
    gap = row_gaps(pts)[None]
    p0 = direction.T
    own = spread(jnp.concatenate([centres, p0.astype(BF)], 0), "ctr")
    other = other_core(own)

    tile, u0 = build(pts, gap, own, None)
    tile_other, u0 = build(pts, gap, other, u0)
    z0 = precondition(factor, residual)
    u0 = reduce_points(u0, [lanes(residual.T, z0.T), lanes(p0, p0)])
    v0, s = reduce_centres(u0, tile, tile_other, 2)
    rz0 = s[0]
    q0 = v0 + RIDGE * p0
    alpha0 = rz0 / (s[2] / total_points + RIDGE * s[1])
    r1 = residual.T - alpha0 * q0
    z1 = precondition(factor, r1.T).T
    block = jnp.stack([lanes(r1, z1), lanes(z1, z1), lanes(z1, p0)] + [jnp.zeros((LANES,), F32)] * (RIDE - 3))
    for axes in ("z", ("core", "ctr")):
        block = jnp.sum(spread(block, axes), axis=0)
    rz1, zz, zp = [jnp.sum(block[k]) for k in range(3)]
    beta = rz1 / rz0
    p1 = z1 + beta * p0
    pp = zz + beta * (2.0 * zp + beta * s[1])

    own = spread(p1.astype(BF), "ctr")
    other = other_core(own)
    u1 = apply(own, tile, None)
    u1 = apply(other, tile_other, u1)
    u1 = reduce_points(u1, [])
    v1, s = reduce_centres(u1, tile, tile_other, 0)
    q1 = v1 + RIDGE * p1
    alpha1 = rz1 / (s[0] / total_points + RIDGE * pp)
    x2 = solution + (alpha0 * p0 + alpha1 * p1).T
    r2 = (r1 - alpha1 * q1).T
    return x2, r2


def solution(mesh):
    shape = (mesh.shape["pt"] // CORES, CORES, mesh.shape["ctr"])
    fine = Mesh(mesh.devices.reshape(shape), ("z", "core", "ctr"))
    rows = P(("z", "core", "ctr"), None)
    return jax.shard_map(
        body,
        mesh=fine,
        in_specs=(P(("z", "core"), None),) + (rows,) * 5,
        out_specs=(rows, rows),
        check_vma=False,
    )
```

```python
import functools
import math

import jax
import jax.numpy as jnp
from jax import lax
from jax.experimental import pallas as pl
from jax.experimental.pallas import tpu as pltpu
from jax.sharding import Mesh, PartitionSpec as P

GAMMA_SCALE = 0.8
RIDGE = 64.0
CORES = 2
LANES = 128
GROUP = 2
ROWS = 16
RIDE = 8
BF = jnp.bfloat16
F32 = jnp.float32
PARAMS = pltpu.CompilerParams(vmem_limit_bytes=52 * 1024 * 1024)


def row_gaps(rows):
    wide = rows.astype(F32)
    return rows.shape[1] - jnp.sum(wide * wide, axis=1)


def precondition(factor, resid):
    lower = lax.linalg.triangular_solve(factor, resid, left_side=True, lower=True)
    return lax.linalg.triangular_solve(factor, lower, left_side=True, lower=True, transpose_a=True)


def exchange(blocks, axes):
    return lax.all_to_all(blocks, axes, 0, 0, tiled=True)


def spread(block, axes):
    count = lax.axis_size(axes)
    return exchange(jnp.broadcast_to(block[None], (count,) + block.shape), axes)


def other_core(block):
    return lax.ppermute(block, "core", [(0, 1), (1, 0)])


def pack(rows):
    pieces = []
    for row in rows:
        for _ in range(3):
            piece = lax.reduce_precision(row, 8, 7)
            pieces.append(piece)
            row = row - piece
    pieces += [jnp.zeros_like(pieces[0])] * (ROWS - len(pieces))
    return jnp.stack(pieces).astype(BF)


def chunks_of(total):
    half = total.shape[0] // 2
    return [
        total[part * half : (part + 1) * half, at : at + LANES]
        for at in range(0, total.shape[1], LANES)
        for part in range(2)
    ]


def add_up(step, part, before_ref, u_ref, acc):
    @pl.when(step == 0)
    def _():
        acc[...] = part

    @pl.when(step > 0)
    def _():
        acc[...] += part

    @pl.when(step == pl.num_programs(0) - 1)
    def _():
        for at, piece in enumerate(chunks_of(acc[...])):
            u_ref[at] = piece if before_ref is None else piece + before_ref[at]


def rows_at(step):
    rows = GROUP * LANES
    return pl.ds(pl.multiple_of(step * rows, rows), rows)


def half_of(tile_ref, half):
    rows = tile_ref.shape[0] // 2
    return tile_ref.at[pl.ds(half * rows, rows)]


def tile_copy(source, target, sems, step):
    rows = rows_at(step)
    return pltpu.make_async_copy(source.at[rows], target.at[rows], sems.at[step])


def fetch(step, tile_ref, buf, sems):
    @pl.when(step == 0)
    def _():
        for at in range(sems.shape[0]):
            tile_copy(tile_ref, buf, sems, at).start()

    tile_copy(tile_ref, buf, sems, step).wait()
    return buf[rows_at(step)]


def build_kernel(gamma, half, pts_ref, gap_ref, blk_ref, *rest):
    before_ref = rest[0] if half else None
    tile_ref, u_ref, acc, buf, sems = rest[-5:]
    tile_ref = half_of(tile_ref, half)
    step = pl.program_id(0)
    dim = pts_ref.shape[1]
    blk = blk_ref[...]
    cen = jnp.concatenate([blk[g, :LANES] for g in range(GROUP)], axis=0)
    vec = jnp.concatenate([blk[g, LANES:] for g in range(GROUP)], axis=1)
    wide = cen.astype(F32)
    gap_c = dim - jnp.sum(wide * wide, axis=1, keepdims=True)
    cross = lax.dot_general(cen, pts_ref[...], (((1,), (1,)), ((), ())), preferred_element_type=F32)
    tile = jnp.exp(gamma * (2.0 * cross + gap_c + gap_ref[...])).astype(BF)
    buf[rows_at(step)] = tile
    tile_copy(buf, tile_ref, sems, step).start()
    part = jnp.dot(vec, tile, preferred_element_type=F32)
    add_up(step, part, before_ref, u_ref, acc)

    @pl.when(step == pl.num_programs(0) - 1)
    def _():
        for at in range(sems.shape[0]):
            tile_copy(buf, tile_ref, sems, at).wait()


def apply_kernel(half, blk_ref, tile_ref, *rest):
    before_ref = rest[0] if half else None
    tile_ref = half_of(tile_ref, half)
    u_ref, acc, buf, sems = rest[-4:]
    step = pl.program_id(0)
    tile = fetch(step, tile_ref, buf, sems)
    blk = blk_ref[...]
    vec = jnp.concatenate([blk[g] for g in range(GROUP)], axis=1)
    part = jnp.dot(vec, tile, preferred_element_type=F32)
    add_up(step, part, before_ref, u_ref, acc)


def back_kernel(half, count, u_ref, tile_ref, v_ref, ub, ride, buf, sems):
    tile_ref = half_of(tile_ref, half)
    outs = ub.shape[0]
    half = outs // 2
    step = pl.program_id(0)
    tile = fetch(step, tile_ref, buf, sems)

    @pl.when(step == 0)
    def _():
        squares = jnp.zeros((half, LANES), F32)
        for at in range(u_ref.shape[0]):
            piece = u_ref[at, :half]
            low = (at % 2) * half
            ub[low : low + half, (at // 2) * LANES : (at // 2 + 1) * LANES] = piece
            squares += piece.astype(F32) * piece.astype(F32)
        packed = jnp.sum(u_ref[:, half:].astype(F32), axis=0) if count else None
        rows = [packed[3 * k : 3 * k + 1] + packed[3 * k + 1 : 3 * k + 2] + packed[3 * k + 2 : 3 * k + 3] for k in range(count)]
        rows.append(jnp.sum(squares, axis=0, keepdims=True))
        rows.append(jnp.zeros((RIDE - count - 1, LANES), F32))
        ride[...] = jnp.concatenate(rows, axis=0)

    v = lax.dot_general(ub[...], tile, (((1,), (1,)), ((), ())), preferred_element_type=F32)
    for g in range(GROUP):
        v_ref[g, :outs] = v[:, g * LANES : (g + 1) * LANES]
        v_ref[g, outs:] = ride[...]


def body(points, centres, factor, solution, residual, direction):
    dim = points.shape[1]
    gamma = GAMMA_SCALE / math.sqrt(dim)
    outs = direction.shape[1]
    n_z, n_ctr = lax.axis_size("z"), lax.axis_size("ctr")
    total_points = points.shape[0] * n_z * CORES
    n_pts = points.shape[0]
    share = n_pts // n_ctr
    grid = (n_ctr // GROUP,)
    u_shape = jax.ShapeDtypeStruct((2 * n_pts // LANES, outs // 2, LANES), F32)
    whole = lambda shape: pl.BlockSpec(shape, lambda i: (0,) * len(shape))
    blocks = lambda rows: pl.BlockSpec((GROUP, rows, LANES), lambda i: (i, 0, 0))
    tiles = pl.BlockSpec(memory_space=pltpu.HBM)
    copies = [pltpu.VMEM((n_ctr * LANES, n_pts), BF), pltpu.SemaphoreType.DMA(grid)]
    acc = pltpu.VMEM((outs, n_pts), F32)
    work = n_ctr * LANES * n_pts

    def cost(flops, exps, size):
        return pl.CostEstimate(flops=flops, transcendentals=exps, bytes_accessed=size)

    def build(pts, gap, blk, before):
        extra = [] if before is None else [before[1], before[0]]
        return pl.pallas_call(
            functools.partial(build_kernel, gamma, len(extra) // 2),
            grid=grid,
            in_specs=[whole(pts.shape), whole(gap.shape), blocks(blk.shape[1])] + [whole(u_shape.shape), tiles][: len(extra)],
            out_specs=[tiles, whole(u_shape.shape)],
            out_shape=[jax.ShapeDtypeStruct((CORES * n_ctr * LANES, n_pts), BF), u_shape],
            input_output_aliases={4: 0} if extra else {},
            scratch_shapes=[acc] + copies,
            compiler_params=PARAMS,
            cost_estimate=cost(2 * work * (dim + outs), work, 2 * work),
            name="build_tile",
        )(pts, gap, blk, *extra)

    def apply(blk, tile, before):
        extra = [] if before is None else [before]
        return pl.pallas_call(
            functools.partial(apply_kernel, len(extra)),
            grid=grid,
            in_specs=[blocks(outs), tiles] + [whole(u_shape.shape)] * len(extra),
            out_specs=whole(u_shape.shape),
            out_shape=u_shape,
            scratch_shapes=[acc] + copies,
            compiler_params=PARAMS,
            cost_estimate=cost(2 * work * outs, 0, 2 * work),
            name="apply_tile",
        )(blk, tile, *extra)

    def back(u, tile, half, count):
        return pl.pallas_call(
            functools.partial(back_kernel, half, count),
            grid=grid,
            in_specs=[whole(u.shape), tiles],
            out_specs=blocks(outs + RIDE),
            out_shape=jax.ShapeDtypeStruct((n_ctr, outs + RIDE, LANES), F32),
            scratch_shapes=[pltpu.VMEM((outs, n_pts), BF), pltpu.VMEM((RIDE, LANES), F32)] + copies,
            compiler_params=PARAMS,
            cost_estimate=cost(2 * work * outs, 0, 2 * work),
            name="back_tile",
        )(u, tile)

    def reduce_points(u, rows):
        u = jnp.sum(exchange(u, "z"), axis=0).astype(BF)
        return spread(jnp.concatenate([u, pack(rows)], 0) if rows else u, "z")

    def reduce_centres(u, tile, count):
        v = other_core(back(u, tile, 1, count))
        v = back(u, tile, 0, count) + v
        v = jnp.sum(exchange(v, "ctr"), axis=0)
        return v[:outs] / total_points, jnp.sum(v[outs : outs + count + 1], axis=1)

    def lanes(left, right):
        return jnp.sum(left * right, axis=0)

    mine = lax.dynamic_slice_in_dim(points, lax.axis_index("ctr") * share, share, 0)
    pts = spread(mine, "z").reshape(n_pts, dim)
    gap = row_gaps(pts)[None]
    p0 = direction.T
    own = spread(jnp.concatenate([centres, p0.astype(BF)], 0), "ctr")
    other = other_core(own)

    tile, u0 = build(pts, gap, other, build(pts, gap, own, None))
    z0 = precondition(factor, residual)
    u0 = reduce_points(u0, [lanes(residual.T, z0.T), lanes(p0, p0)])
    v0, s = reduce_centres(u0, tile, 2)
    rz0 = s[0]
    q0 = v0 + RIDGE * p0
    alpha0 = rz0 / (s[2] / total_points + RIDGE * s[1])
    r1 = residual.T - alpha0 * q0
    z1 = precondition(factor, r1.T).T
    block = jnp.stack([lanes(r1, z1), lanes(z1, z1), lanes(z1, p0)] + [jnp.zeros((LANES,), F32)] * (RIDE - 3))
    for axes in ("z", ("core", "ctr")):
        block = jnp.sum(spread(block, axes), axis=0)
    rz1, zz, zp = [jnp.sum(block[k]) for k in range(3)]
    beta = rz1 / rz0
    p1 = z1 + beta * p0
    pp = zz + beta * (2.0 * zp + beta * s[1])

    own = spread(p1.astype(BF), "ctr")
    other = other_core(own)
    u1 = apply(own, tile, None)
    u1 = apply(other, tile, u1)
    u1 = reduce_points(u1, [])
    v1, s = reduce_centres(u1, tile, 0)
    q1 = v1 + RIDGE * p1
    alpha1 = rz1 / (s[0] / total_points + RIDGE * pp)
    x2 = solution + (alpha0 * p0 + alpha1 * p1).T
    r2 = (r1 - alpha1 * q1).T
    return x2, r2


def solution(mesh):
    shape = (mesh.shape["pt"] // CORES, CORES, mesh.shape["ctr"])
    fine = Mesh(mesh.devices.reshape(shape), ("z", "core", "ctr"))
    rows = P(("z", "core", "ctr"), None)
    return jax.shard_map(
        body,
        mesh=fine,
        in_specs=(P(("z", "core"), None),) + (rows,) * 5,
        out_specs=(rows, rows),
        check_vma=False,
    )
```

```python
import functools
import math

import jax
import jax.numpy as jnp
from jax import lax
from jax.experimental import pallas as pl
from jax.experimental.pallas import tpu as pltpu
from jax.sharding import Mesh, PartitionSpec as P

GAMMA_SCALE = 0.8
RIDGE = 64.0
CORES = 2
LANES = 128
GROUP = 2
ROWS = 16
RIDE = 8
BF = jnp.bfloat16
F32 = jnp.float32
PARAMS = pltpu.CompilerParams(vmem_limit_bytes=52 * 1024 * 1024)


def row_gaps(rows):
    wide = rows.astype(F32)
    return rows.shape[1] - jnp.sum(wide * wide, axis=1)


def precondition(factor, resid):
    lower = lax.linalg.triangular_solve(factor, resid, left_side=True, lower=True)
    return lax.linalg.triangular_solve(factor, lower, left_side=True, lower=True, transpose_a=True)


def exchange(blocks, axes):
    return lax.all_to_all(blocks, axes, 0, 0, tiled=True)


def spread(block, axes):
    count = lax.axis_size(axes)
    return exchange(jnp.broadcast_to(block[None], (count,) + block.shape), axes)


def other_core(block):
    return lax.ppermute(block, "core", [(0, 1), (1, 0)])


def pack(rows):
    pieces = []
    for row in rows:
        for _ in range(3):
            piece = lax.reduce_precision(row, 8, 7)
            pieces.append(piece)
            row = row - piece
    pieces += [jnp.zeros_like(pieces[0])] * (ROWS - len(pieces))
    return jnp.stack(pieces).astype(BF)


def chunks_of(total):
    half = total.shape[0] // 2
    return [
        total[part * half : (part + 1) * half, at : at + LANES]
        for at in range(0, total.shape[1], LANES)
        for part in range(2)
    ]


def add_up(step, part, before_ref, u_ref, acc):
    @pl.when(step == 0)
    def _():
        acc[...] = part

    @pl.when(step > 0)
    def _():
        acc[...] += part

    @pl.when(step == pl.num_programs(0) - 1)
    def _():
        for at, piece in enumerate(chunks_of(acc[...])):
            u_ref[at] = piece if before_ref is None else piece + before_ref[at]


def rows_at(step):
    rows = GROUP * LANES
    return pl.ds(pl.multiple_of(step * rows, rows), rows)


def half_of(tile_ref, half):
    rows = tile_ref.shape[0] // 2
    return tile_ref.at[pl.ds(half * rows, rows)]


def tile_copy(source, target, sems, step):
    rows = rows_at(step)
    return pltpu.make_async_copy(source.at[rows], target.at[rows], sems.at[step])


def fetch(step, tile_ref, buf, sems):
    @pl.when(step == 0)
    def _():
        for at in range(sems.shape[0]):
            tile_copy(tile_ref, buf, sems, at).start()

    tile_copy(tile_ref, buf, sems, step).wait()
    return buf[rows_at(step)]


def build_kernel(gamma, half, pts_ref, gap_ref, blk_ref, *rest):
    before_ref = rest[0] if half else None
    tile_ref, u_ref, acc, buf, sems = rest[-5:]
    tile_ref = half_of(tile_ref, half)
    step = pl.program_id(0)
    dim = pts_ref.shape[1]
    outs = acc.shape[0]
    blk = blk_ref[...]
    cen = jnp.concatenate([blk[g, :LANES] for g in range(GROUP)], axis=0)
    vec = jnp.concatenate([blk[g, LANES : LANES + outs] for g in range(GROUP)], axis=1)
    wide = cen.astype(F32)
    gap_c = dim - jnp.sum(wide * wide, axis=1, keepdims=True)
    cross = lax.dot_general(cen, pts_ref[...], (((1,), (1,)), ((), ())), preferred_element_type=F32)
    tile = jnp.exp(gamma * (2.0 * cross + gap_c + gap_ref[...])).astype(BF)
    buf[rows_at(step)] = tile
    tile_copy(buf, tile_ref, sems, step).start()
    part = jnp.dot(vec, tile, preferred_element_type=F32)
    add_up(step, part, before_ref, u_ref, acc)

    @pl.when(step == pl.num_programs(0) - 1)
    def _():
        for at in range(sems.shape[0]):
            tile_copy(buf, tile_ref, sems, at).wait()


def apply_kernel(half, beta_ref, z_ref, p_ref, tile_ref, *rest):
    before_ref = rest[0] if half else None
    tile_ref = half_of(tile_ref, half)
    u_ref, acc, buf, sems = rest[-4:]
    step = pl.program_id(0)
    tile = fetch(step, tile_ref, buf, sems)
    outs = acc.shape[0]
    vec = []
    for g in range(GROUP):
        high = p_ref[g, LANES : LANES + outs].astype(F32)
        low = p_ref[g, LANES + outs :].astype(F32)
        vec.append((z_ref[g, :outs] + beta_ref[...] * (high + low)).astype(BF))
    part = jnp.dot(jnp.concatenate(vec, axis=1), tile, preferred_element_type=F32)
    add_up(step, part, before_ref, u_ref, acc)


def back_kernel(half, count, u_ref, tile_ref, v_ref, ub, ride, buf, sems):
    tile_ref = half_of(tile_ref, half)
    outs = ub.shape[0]
    half = outs // 2
    step = pl.program_id(0)
    tile = fetch(step, tile_ref, buf, sems)

    @pl.when(step == 0)
    def _():
        squares = jnp.zeros((half, LANES), F32)
        for at in range(u_ref.shape[0]):
            piece = u_ref[at, :half]
            low = (at % 2) * half
            ub[low : low + half, (at // 2) * LANES : (at // 2 + 1) * LANES] = piece
            squares += piece.astype(F32) * piece.astype(F32)
        packed = jnp.sum(u_ref[:, half:].astype(F32), axis=0) if count else None
        rows = [packed[3 * k : 3 * k + 1] + packed[3 * k + 1 : 3 * k + 2] + packed[3 * k + 2 : 3 * k + 3] for k in range(count)]
        rows.append(jnp.sum(squares, axis=0, keepdims=True))
        rows.append(jnp.zeros((RIDE - count - 1, LANES), F32))
        ride[...] = jnp.concatenate(rows, axis=0)

    v = lax.dot_general(ub[...], tile, (((1,), (1,)), ((), ())), preferred_element_type=F32)
    for g in range(GROUP):
        v_ref[g, :outs] = v[:, g * LANES : (g + 1) * LANES]
        v_ref[g, outs:] = ride[...]


def body(points, centres, factor, solution, residual, direction):
    dim = points.shape[1]
    gamma = GAMMA_SCALE / math.sqrt(dim)
    outs = direction.shape[1]
    n_z, n_ctr = lax.axis_size("z"), lax.axis_size("ctr")
    total_points = points.shape[0] * n_z * CORES
    n_pts = points.shape[0]
    share = n_pts // n_ctr
    grid = (n_ctr // GROUP,)
    u_shape = jax.ShapeDtypeStruct((2 * n_pts // LANES, outs // 2, LANES), F32)
    whole = lambda shape: pl.BlockSpec(shape, lambda i: (0,) * len(shape))
    blocks = lambda rows: pl.BlockSpec((GROUP, rows, LANES), lambda i: (i, 0, 0))
    tiles = pl.BlockSpec(memory_space=pltpu.HBM)
    copies = [pltpu.VMEM((n_ctr * LANES, n_pts), BF), pltpu.SemaphoreType.DMA(grid)]
    acc = pltpu.VMEM((outs, n_pts), F32)
    work = n_ctr * LANES * n_pts

    def cost(flops, exps, size):
        return pl.CostEstimate(flops=flops, transcendentals=exps, bytes_accessed=size)

    def build(pts, gap, blk, before):
        extra = [] if before is None else [before[1], before[0]]
        return pl.pallas_call(
            functools.partial(build_kernel, gamma, len(extra) // 2),
            grid=grid,
            in_specs=[whole(pts.shape), whole(gap.shape), blocks(blk.shape[1])] + [whole(u_shape.shape), tiles][: len(extra)],
            out_specs=[tiles, whole(u_shape.shape)],
            out_shape=[jax.ShapeDtypeStruct((CORES * n_ctr * LANES, n_pts), BF), u_shape],
            input_output_aliases={4: 0} if extra else {},
            scratch_shapes=[acc] + copies,
            compiler_params=PARAMS,
            cost_estimate=cost(2 * work * (dim + outs), work, 2 * work),
            name="build_tile",
        )(pts, gap, blk, *extra)

    def apply(beta, z, p, tile, before):
        extra = [] if before is None else [before]
        return pl.pallas_call(
            functools.partial(apply_kernel, len(extra)),
            grid=grid,
            in_specs=[whole(beta.shape), blocks(z.shape[1]), blocks(p.shape[1]), tiles] + [whole(u_shape.shape)] * len(extra),
            out_specs=whole(u_shape.shape),
            out_shape=u_shape,
            scratch_shapes=[acc] + copies,
            compiler_params=PARAMS,
            cost_estimate=cost(2 * work * outs, 0, 2 * work),
            name="apply_tile",
        )(beta, z, p, tile, *extra)

    def back(u, tile, half, count):
        return pl.pallas_call(
            functools.partial(back_kernel, half, count),
            grid=grid,
            in_specs=[whole(u.shape), tiles],
            out_specs=blocks(outs + RIDE),
            out_shape=jax.ShapeDtypeStruct((n_ctr, outs + RIDE, LANES), F32),
            scratch_shapes=[pltpu.VMEM((outs, n_pts), BF), pltpu.VMEM((RIDE, LANES), F32)] + copies,
            compiler_params=PARAMS,
            cost_estimate=cost(2 * work * outs, 0, 2 * work),
            name="back_tile",
        )(u, tile)

    def reduce_points(u, rows):
        u = jnp.sum(exchange(u, "z"), axis=0).astype(BF)
        return spread(jnp.concatenate([u, pack(rows)], 0) if rows else u, "z")

    def reduce_centres(u, tile, count):
        v = other_core(back(u, tile, 1, count))
        v = back(u, tile, 0, count) + v
        v = jnp.sum(exchange(v, "ctr"), axis=0)
        return v[:outs] / total_points, jnp.sum(v[outs : outs + count + 1], axis=1)

    def lanes(left, right):
        return jnp.sum(left * right, axis=0)

    mine = lax.dynamic_slice_in_dim(points, lax.axis_index("ctr") * share, share, 0)
    pts = spread(mine, "z").reshape(n_pts, dim)
    gap = row_gaps(pts)[None]
    p0 = direction.T
    p0_high = lax.reduce_precision(p0, 8, 7)
    parts = [centres, p0_high.astype(BF), (p0 - p0_high).astype(BF)]
    own = spread(jnp.concatenate(parts, 0), "ctr")
    other = other_core(own)

    tile, u0 = build(pts, gap, other, build(pts, gap, own, None))
    z0 = precondition(factor, residual)
    u0 = reduce_points(u0, [lanes(residual.T, z0.T), lanes(p0, p0)])
    v0, s = reduce_centres(u0, tile, 2)
    rz0 = s[0]
    q0 = v0 + RIDGE * p0
    alpha0 = rz0 / (s[2] / total_points + RIDGE * s[1])
    r1 = residual.T - alpha0 * q0
    z1 = precondition(factor, r1.T).T
    zeros = [jnp.zeros((LANES,), F32)] * (RIDE - 3)
    block = jnp.stack([lanes(r1, z1), lanes(z1, z1), lanes(z1, p0)] + zeros)
    own_z = spread(jnp.concatenate([z1, block], 0), "ctr")
    other_z = other_core(own_z)
    block = jnp.sum(spread(jnp.sum(own_z[:, outs:], axis=0), ("z", "core")), axis=0)
    rz1, zz, zp = [jnp.sum(block[k]) for k in range(3)]
    beta = rz1 / rz0
    p1 = z1 + beta * p0
    pp = zz + beta * (2.0 * zp + beta * s[1])

    rate = jnp.broadcast_to(beta, (1, LANES))
    u1 = apply(rate, own_z, own, tile, None)
    u1 = apply(rate, other_z, other, tile, u1)
    u1 = reduce_points(u1, [])
    v1, s = reduce_centres(u1, tile, 0)
    q1 = v1 + RIDGE * p1
    alpha1 = rz1 / (s[0] / total_points + RIDGE * pp)
    x2 = solution + (alpha0 * p0 + alpha1 * p1).T
    r2 = (r1 - alpha1 * q1).T
    return x2, r2


def solution(mesh):
    shape = (mesh.shape["pt"] // CORES, CORES, mesh.shape["ctr"])
    fine = Mesh(mesh.devices.reshape(shape), ("z", "core", "ctr"))
    rows = P(("z", "core", "ctr"), None)
    return jax.shard_map(
        body,
        mesh=fine,
        in_specs=(P(("z", "core"), None),) + (rows,) * 5,
        out_specs=(rows, rows),
        check_vma=False,
    )
```

```python
import functools
import math

import jax
import jax.numpy as jnp
from jax import lax
from jax.experimental import pallas as pl
from jax.experimental.pallas import tpu as pltpu
from jax.sharding import Mesh, PartitionSpec as P

GAMMA_SCALE = 0.8
RIDGE = 64.0
CORES = 2
LANES = 128
GROUP = 2
ROWS = 16
RIDE = 8
BF = jnp.bfloat16
F32 = jnp.float32
PARAMS = pltpu.CompilerParams(vmem_limit_bytes=52 * 1024 * 1024)


def precondition(factor, resid):
    lower = lax.linalg.triangular_solve(factor, resid, left_side=True, lower=True)
    return lax.linalg.triangular_solve(factor, lower, left_side=True, lower=True, transpose_a=True)


def exchange(blocks, axes):
    return lax.all_to_all(blocks, axes, 0, 0, tiled=True)


def spread(block, axes):
    count = lax.axis_size(axes)
    return exchange(jnp.broadcast_to(block[None], (count,) + block.shape), axes)


def other_core(block):
    return lax.ppermute(block, "core", [(0, 1), (1, 0)])


def pack(rows):
    pieces = []
    for row in rows:
        for _ in range(3):
            piece = lax.reduce_precision(row, 8, 7)
            pieces.append(piece)
            row = row - piece
    pieces += [jnp.zeros_like(pieces[0])] * (ROWS - len(pieces))
    return jnp.stack(pieces).astype(BF)


def chunks_of(total):
    half = total.shape[0] // 2
    return [
        total[part * half : (part + 1) * half, at : at + LANES]
        for at in range(0, total.shape[1], LANES)
        for part in range(2)
    ]


def add_up(step, part, u_ref, acc):
    @pl.when(step == 0)
    def _():
        acc[...] = part

    @pl.when(step > 0)
    def _():
        acc[...] += part

    @pl.when(step == pl.num_programs(0) - 1)
    def _():
        for at, piece in enumerate(chunks_of(acc[...])):
            u_ref[at] = piece


def rows_at(step):
    rows = GROUP * LANES
    return pl.ds(pl.multiple_of(step * rows, rows), rows)


def tile_copy(source, target, sems, step):
    rows = rows_at(step)
    return pltpu.make_async_copy(source.at[rows], target.at[rows], sems.at[step])


def fetch(steps, tile_ref, buf, sems):
    @pl.when(pl.program_id(0) == 0)
    def _():
        for at in range(sems.shape[0]):
            tile_copy(tile_ref, buf, sems, at).start()

    for step in steps:
        tile_copy(tile_ref, buf, sems, step).wait()
    return [buf[rows_at(step)] for step in steps]


def gap_columns(rows, place):
    wide = rows.astype(F32)
    left = 0.5 * (rows.shape[1] - jnp.sum(wide * wide, axis=1, keepdims=True))
    lane = lax.broadcasted_iota(jnp.int32, (rows.shape[0], LANES), 1)
    columns = jnp.where(lane < 6, 1.0, 0.0)
    for k in range(3):
        piece = left.astype(BF).astype(F32)
        columns = jnp.where(lane == place + k, piece, columns)
        left = left - piece
    return columns.astype(BF)


def build_kernel(gamma, pts_ref, own_ref, other_ref, tile_ref, u_ref, acc, buf, sems, side):
    step = pl.program_id(0)
    steps = pl.num_programs(0)
    outs = acc.shape[0]

    @pl.when(step == 0)
    def _():
        side[...] = gap_columns(pts_ref[...], 3)

    pts = jnp.concatenate([pts_ref[...], side[...]], axis=1)
    part = None
    for blk_ref, place in ((own_ref, step), (other_ref, step + steps)):
        cen = jnp.concatenate([blk_ref[g, :LANES] for g in range(GROUP)], axis=0)
        vec = jnp.concatenate([blk_ref[g, LANES : LANES + outs] for g in range(GROUP)], axis=1)
        cen = jnp.concatenate([cen, gap_columns(cen, 0)], axis=1)
        cross = lax.dot_general(cen, pts, (((1,), (1,)), ((), ())), preferred_element_type=F32)
        tile = jnp.exp2((2.0 * gamma * math.log2(math.e)) * cross).astype(BF)
        buf[rows_at(place)] = tile
        tile_copy(buf, tile_ref, sems, place).start()
        term = jnp.dot(vec, tile, preferred_element_type=F32)
        part = term if part is None else part + term
    add_up(step, part, u_ref, acc)

    @pl.when(step == steps - 1)
    def _():
        for at in range(sems.shape[0]):
            tile_copy(buf, tile_ref, sems, at).wait()


def apply_kernel(beta_ref, z_ref, p_ref, z_other_ref, p_other_ref, tile_ref, u_ref, acc, buf, sems):
    step = pl.program_id(0)
    outs = acc.shape[0]
    tiles = fetch([step, step + pl.num_programs(0)], tile_ref, buf, sems)
    part = None
    for tile, z, p in zip(tiles, (z_ref, z_other_ref), (p_ref, p_other_ref)):
        vec = []
        for g in range(GROUP):
            high = p[g, LANES : LANES + outs].astype(F32)
            low = p[g, LANES + outs :].astype(F32)
            vec.append((z[g, :outs] + beta_ref[...] * (high + low)).astype(BF))
        term = jnp.dot(jnp.concatenate(vec, axis=1), tile, preferred_element_type=F32)
        part = term if part is None else part + term
    add_up(step, part, u_ref, acc)


def back_kernel(half, count, u_ref, tile_ref, v_ref, ub, ride, buf, sems):
    rows = buf.shape[0]
    outs = ub.shape[0]
    step = pl.program_id(0)
    tile = fetch([step], tile_ref.at[pl.ds(half * rows, rows)], buf, sems)[0]
    half = outs // 2

    @pl.when(step == 0)
    def _():
        squares = jnp.zeros((half, LANES), F32)
        for at in range(u_ref.shape[0]):
            piece = u_ref[at, :half]
            low = (at % 2) * half
            ub[low : low + half, (at // 2) * LANES : (at // 2 + 1) * LANES] = piece
            squares += piece.astype(F32) * piece.astype(F32)
        packed = jnp.sum(u_ref[:, half:].astype(F32), axis=0) if count else None
        rows = [packed[3 * k : 3 * k + 1] + packed[3 * k + 1 : 3 * k + 2] + packed[3 * k + 2 : 3 * k + 3] for k in range(count)]
        rows.append(jnp.sum(squares, axis=0, keepdims=True))
        rows.append(jnp.zeros((RIDE - count - 1, LANES), F32))
        ride[...] = jnp.concatenate(rows, axis=0)

    v = lax.dot_general(ub[...], tile, (((1,), (1,)), ((), ())), preferred_element_type=F32)
    for g in range(GROUP):
        v_ref[g, :outs] = v[:, g * LANES : (g + 1) * LANES]
        v_ref[g, outs:] = ride[...]


def body(points, centres, factor, solution, residual, direction):
    dim = points.shape[1]
    gamma = GAMMA_SCALE / math.sqrt(dim)
    outs = direction.shape[1]
    n_z, n_ctr = lax.axis_size("z"), lax.axis_size("ctr")
    total_points = points.shape[0] * n_z * CORES
    n_pts = points.shape[0]
    share = n_pts // n_ctr
    grid = (n_ctr // GROUP,)
    u_shape = jax.ShapeDtypeStruct((2 * n_pts // LANES, outs // 2, LANES), F32)
    whole = lambda shape: pl.BlockSpec(shape, lambda i: (0,) * len(shape))
    blocks = lambda rows: pl.BlockSpec((GROUP, rows, LANES), lambda i: (i, 0, 0))
    tiles = pl.BlockSpec(memory_space=pltpu.HBM)

    def copies(halves):
        return [pltpu.VMEM((halves * n_ctr * LANES, n_pts), BF), pltpu.SemaphoreType.DMA((halves * grid[0],))]
    acc = pltpu.VMEM((outs, n_pts), F32)
    work = n_ctr * LANES * n_pts

    def cost(flops, exps, size):
        return pl.CostEstimate(flops=flops, transcendentals=exps, bytes_accessed=size)

    def build(pts, own, other):
        return pl.pallas_call(
            functools.partial(build_kernel, gamma),
            grid=grid,
            in_specs=[whole(pts.shape), blocks(own.shape[1]), blocks(own.shape[1])],
            out_specs=[tiles, whole(u_shape.shape)],
            out_shape=[jax.ShapeDtypeStruct((CORES * n_ctr * LANES, n_pts), BF), u_shape],
            scratch_shapes=[acc] + copies(CORES) + [pltpu.VMEM((n_pts, LANES), BF)],
            compiler_params=PARAMS,
            cost_estimate=cost(4 * work * (dim + outs), 2 * work, 4 * work),
            name="build_tile",
        )(pts, own, other)

    def apply(beta, z, p, z_other, p_other, tile):
        return pl.pallas_call(
            apply_kernel,
            grid=grid,
            in_specs=[whole(beta.shape)] + [blocks(z.shape[1]), blocks(p.shape[1])] * 2 + [tiles],
            out_specs=whole(u_shape.shape),
            out_shape=u_shape,
            scratch_shapes=[acc] + copies(CORES),
            compiler_params=PARAMS,
            cost_estimate=cost(4 * work * outs, 0, 4 * work),
            name="apply_tile",
        )(beta, z, p, z_other, p_other, tile)

    def back(u, tile, half, count):
        return pl.pallas_call(
            functools.partial(back_kernel, half, count),
            grid=grid,
            in_specs=[whole(u.shape), tiles],
            out_specs=blocks(outs + RIDE),
            out_shape=jax.ShapeDtypeStruct((n_ctr, outs + RIDE, LANES), F32),
            scratch_shapes=[pltpu.VMEM((outs, n_pts), BF), pltpu.VMEM((RIDE, LANES), F32)] + copies(1),
            compiler_params=PARAMS,
            cost_estimate=cost(2 * work * outs, 0, 2 * work),
            name="back_tile",
        )(u, tile)

    def reduce_points(u, rows):
        u = jnp.sum(exchange(u, "z"), axis=0).astype(BF)
        return spread(jnp.concatenate([u, pack(rows)], 0) if rows else u, "z")

    def reduce_centres(u, tile, count):
        v = other_core(back(u, tile, 1, count))
        v = back(u, tile, 0, count) + v
        v = jnp.sum(exchange(v, "ctr"), axis=0)
        return v[:outs] / total_points, jnp.sum(v[outs : outs + count + 1], axis=1)

    def lanes(left, right):
        return jnp.sum(left * right, axis=0)

    mine = lax.dynamic_slice_in_dim(points, lax.axis_index("ctr") * share, share, 0)
    pts = spread(mine, "z").reshape(n_pts, dim)
    p0 = direction.T
    p0_high = lax.reduce_precision(p0, 8, 7)
    parts = [centres, p0_high.astype(BF), (p0 - p0_high).astype(BF)]
    own = spread(jnp.concatenate(parts, 0), "ctr")
    other = other_core(own)

    tile, u0 = build(pts, own, other)
    z0 = precondition(factor, residual)
    u0 = reduce_points(u0, [lanes(residual.T, z0.T), lanes(p0, p0)])
    v0, s = reduce_centres(u0, tile, 2)
    rz0 = s[0]
    q0 = v0 + RIDGE * p0
    alpha0 = rz0 / (s[2] / total_points + RIDGE * s[1])
    r1 = residual.T - alpha0 * q0
    z1 = precondition(factor, r1.T).T
    zeros = [jnp.zeros((LANES,), F32)] * (RIDE - 3)
    block = jnp.stack([lanes(r1, z1), lanes(z1, z1), lanes(z1, p0)] + zeros)
    block = block + other_core(block)
    own_z = spread(jnp.concatenate([z1, block], 0), "ctr")
    other_z = other_core(own_z)
    block = jnp.sum(spread(jnp.sum(own_z[:, outs:], axis=0), "z"), axis=0)
    rz1, zz, zp = [jnp.sum(block[k]) for k in range(3)]
    beta = rz1 / rz0
    p1 = z1 + beta * p0
    pp = zz + beta * (2.0 * zp + beta * s[1])

    rate = jnp.broadcast_to(beta, (1, LANES))
    u1 = apply(rate, own_z, own, other_z, other, tile)
    u1 = reduce_points(u1, [])
    v1, s = reduce_centres(u1, tile, 0)
    q1 = v1 + RIDGE * p1
    alpha1 = rz1 / (s[0] / total_points + RIDGE * pp)
    x2 = solution + (alpha0 * p0 + alpha1 * p1).T
    r2 = (r1 - alpha1 * q1).T
    return x2, r2


def solution(mesh):
    shape = (mesh.shape["pt"] // CORES, CORES, mesh.shape["ctr"])
    fine = Mesh(mesh.devices.reshape(shape), ("z", "core", "ctr"))
    rows = P(("z", "core", "ctr"), None)
    return jax.shard_map(
        body,
        mesh=fine,
        in_specs=(P(("z", "core"), None),) + (rows,) * 5,
        out_specs=(rows, rows),
        check_vma=False,
    )
```

```python
import functools
import math

import jax
import jax.numpy as jnp
from jax import lax
from jax.experimental import pallas as pl
from jax.experimental.pallas import tpu as pltpu
from jax.sharding import Mesh, PartitionSpec as P

GAMMA_SCALE = 0.8
RIDGE = 64.0
CORES = 2
LANES = 128
GROUP = 2
ROWS = 16
RIDE = 8
BF = jnp.bfloat16
F32 = jnp.float32
SMALL = pltpu.CompilerParams(vmem_limit_bytes=8 * 1024 * 1024)
PARAMS = pltpu.CompilerParams(vmem_limit_bytes=52 * 1024 * 1024)


def precondition(factor, resid):
    lower = lax.linalg.triangular_solve(factor, resid, left_side=True, lower=True)
    return lax.linalg.triangular_solve(factor, lower, left_side=True, lower=True, transpose_a=True)


def exchange(blocks, axes):
    return lax.all_to_all(blocks, axes, 0, 0, tiled=True)


def spread(block, axes):
    count = lax.axis_size(axes)
    return exchange(jnp.broadcast_to(block[None], (count,) + block.shape), axes)


def other_core(block):
    return lax.ppermute(block, "core", [(0, 1), (1, 0)])


def pack(rows):
    pieces = []
    for row in rows:
        for _ in range(3):
            piece = lax.reduce_precision(row, 8, 7)
            pieces.append(piece)
            row = row - piece
    pieces += [jnp.zeros_like(pieces[0])] * (ROWS - len(pieces))
    return jnp.stack(pieces).astype(BF)


def chunks_of(total):
    half = total.shape[0] // 2
    return [
        total[part * half : (part + 1) * half, at : at + LANES]
        for at in range(0, total.shape[1], LANES)
        for part in range(2)
    ]


def add_up(step, part, u_ref, acc):
    @pl.when(step == 0)
    def _():
        acc[...] = part

    @pl.when(step > 0)
    def _():
        acc[...] += part

    @pl.when(step == pl.num_programs(0) - 1)
    def _():
        for at, piece in enumerate(chunks_of(acc[...])):
            u_ref[at] = piece


def rows_at(step):
    rows = GROUP * LANES
    return pl.ds(pl.multiple_of(step * rows, rows), rows)


def tile_copy(source, target, sems, step):
    rows = rows_at(step)
    return pltpu.make_async_copy(source.at[rows], target.at[rows], sems.at[step])


def fetch(steps, tile_ref, buf, sems):
    @pl.when(pl.program_id(0) == 0)
    def _():
        for at in range(sems.shape[0]):
            tile_copy(tile_ref, buf, sems, at).start()

    for step in steps:
        tile_copy(tile_ref, buf, sems, step).wait()
    return [buf[rows_at(step)] for step in steps]


def gap_columns(rows, place):
    wide = rows.astype(F32)
    left = 0.5 * (rows.shape[1] - jnp.sum(wide * wide, axis=1, keepdims=True))
    lane = lax.broadcasted_iota(jnp.int32, (rows.shape[0], LANES), 1)
    columns = jnp.where(lane < 6, 1.0, 0.0)
    for k in range(3):
        piece = left.astype(BF).astype(F32)
        columns = jnp.where(lane == place + k, piece, columns)
        left = left - piece
    return columns.astype(BF)


def build_kernel(gamma, pts_ref, own_ref, other_ref, tile_ref, u_ref, acc, buf, sems, side):
    step = pl.program_id(0)
    steps = pl.num_programs(0)
    outs = acc.shape[0]

    @pl.when(step == 0)
    def _():
        side[...] = gap_columns(pts_ref[...], 3)

    pts = jnp.concatenate([pts_ref[...], side[...]], axis=1)
    part = None
    for blk_ref, place in ((own_ref, step), (other_ref, step + steps)):
        cen = jnp.concatenate([blk_ref[g, :LANES] for g in range(GROUP)], axis=0)
        vec = jnp.concatenate([blk_ref[g, LANES : LANES + outs] for g in range(GROUP)], axis=1)
        cen = jnp.concatenate([cen, gap_columns(cen, 0)], axis=1)
        cross = lax.dot_general(cen, pts, (((1,), (1,)), ((), ())), preferred_element_type=F32)
        tile = jnp.exp2((2.0 * gamma * math.log2(math.e)) * cross).astype(BF)
        buf[rows_at(place)] = tile
        tile_copy(buf, tile_ref, sems, place).start()
        term = jnp.dot(vec, tile, preferred_element_type=F32)
        part = term if part is None else part + term
    add_up(step, part, u_ref, acc)

    @pl.when(step == steps - 1)
    def _():
        for at in range(sems.shape[0]):
            tile_copy(buf, tile_ref, sems, at).wait()


def apply_kernel(sums_ref, scalars_ref, z_ref, p_ref, z_other_ref, p_other_ref, tile_ref, u_ref, acc, buf, sems, beta):
    step = pl.program_id(0)
    outs = acc.shape[0]
    tiles = fetch([step, step + pl.num_programs(0)], tile_ref, buf, sems)

    @pl.when(step == 0)
    def _():
        rate = totals(sums_ref)[0:1] / scalars_ref[0:1, 0:1]
        beta[...] = jnp.broadcast_to(rate, beta.shape)

    part = None
    for tile, z, p in zip(tiles, (z_ref, z_other_ref), (p_ref, p_other_ref)):
        vec = []
        for g in range(GROUP):
            high = p[g, LANES : LANES + outs].astype(F32)
            low = p[g, LANES + outs :].astype(F32)
            vec.append((z[g, :outs] + beta[...] * (high + low)).astype(BF))
        term = jnp.dot(jnp.concatenate(vec, axis=1), tile, preferred_element_type=F32)
        part = term if part is None else part + term
    add_up(step, part, u_ref, acc)


def back_kernel(half, count, u_ref, tile_ref, v_ref, ub, ride, buf, sems):
    rows = buf.shape[0]
    outs = ub.shape[0]
    step = pl.program_id(0)
    tile = fetch([step], tile_ref.at[pl.ds(half * rows, rows)], buf, sems)[0]
    half = outs // 2

    @pl.when(step == 0)
    def _():
        squares = jnp.zeros((half, LANES), F32)
        for at in range(u_ref.shape[0]):
            piece = u_ref[at, :half]
            low = (at % 2) * half
            ub[low : low + half, (at // 2) * LANES : (at // 2 + 1) * LANES] = piece
            squares += piece.astype(F32) * piece.astype(F32)
        packed = jnp.sum(u_ref[:, half:].astype(F32), axis=0) if count else None
        rows = [packed[3 * k : 3 * k + 1] + packed[3 * k + 1 : 3 * k + 2] + packed[3 * k + 2 : 3 * k + 3] for k in range(count)]
        rows.append(jnp.sum(squares, axis=0, keepdims=True))
        rows.append(jnp.zeros((RIDE - count - 1, LANES), F32))
        ride[...] = jnp.concatenate(rows, axis=0)

    v = lax.dot_general(ub[...], tile, (((1,), (1,)), ((), ())), preferred_element_type=F32)
    for g in range(GROUP):
        v_ref[g, :outs] = v[:, g * LANES : (g + 1) * LANES]
        v_ref[g, outs:] = ride[...]


def totals(sums_ref):
    return jnp.sum(jnp.sum(sums_ref[...], axis=0), axis=1, keepdims=True)


def first_kernel(points, v_ref, p_ref, r_ref, r1_ref, scalars_ref):
    outs = p_ref.shape[0]
    v = jnp.sum(v_ref[...], axis=0)
    s = jnp.sum(v[outs:], axis=1, keepdims=True)
    alpha = s[0:1] / (s[2:3] / points + RIDGE * s[1:2])
    r1_ref[...] = r_ref[...] - alpha * (v[:outs] / points + RIDGE * p_ref[...])
    rows = [jnp.broadcast_to(value, (1, LANES)) for value in (s[0:1], s[1:2], alpha)]
    scalars_ref[...] = jnp.concatenate(rows + [jnp.zeros((RIDE - 3, LANES), F32)], axis=0)


def last_kernel(points, v_ref, sums_ref, scalars_ref, z_ref, p_ref, r_ref, x_ref, x_out, r_out):
    outs = p_ref.shape[0]
    v = jnp.sum(v_ref[...], axis=0)
    uu = jnp.sum(v[outs : outs + 1], axis=1, keepdims=True)
    t = totals(sums_ref)
    rz0, pp0, alpha0 = [scalars_ref[k : k + 1, 0:1] for k in range(3)]
    beta = t[0:1] / rz0
    p1 = z_ref[...] + beta * p_ref[...]
    pp = t[1:2] + beta * (2.0 * t[2:3] + beta * pp0)
    alpha1 = t[0:1] / (uu / points + RIDGE * pp)
    x_out[...] = x_ref[...] + alpha0 * p_ref[...] + alpha1 * p1
    r_out[...] = r_ref[...] - alpha1 * (v[:outs] / points + RIDGE * p1)


def body(points, centres, factor, solution, residual, direction):
    dim = points.shape[1]
    gamma = GAMMA_SCALE / math.sqrt(dim)
    outs = direction.shape[1]
    n_z, n_ctr = lax.axis_size("z"), lax.axis_size("ctr")
    total_points = points.shape[0] * n_z * CORES
    n_pts = points.shape[0]
    share = n_pts // n_ctr
    grid = (n_ctr // GROUP,)
    u_shape = jax.ShapeDtypeStruct((2 * n_pts // LANES, outs // 2, LANES), F32)
    whole = lambda shape: pl.BlockSpec(shape, lambda i: (0,) * len(shape))
    blocks = lambda rows: pl.BlockSpec((GROUP, rows, LANES), lambda i: (i, 0, 0))
    tiles = pl.BlockSpec(memory_space=pltpu.HBM)

    def copies(halves):
        return [pltpu.VMEM((halves * n_ctr * LANES, n_pts), BF), pltpu.SemaphoreType.DMA((halves * grid[0],))]
    acc = pltpu.VMEM((outs, n_pts), F32)
    work = n_ctr * LANES * n_pts

    def cost(flops, exps, size):
        return pl.CostEstimate(flops=flops, transcendentals=exps, bytes_accessed=size)

    def build(pts, own, other):
        return pl.pallas_call(
            functools.partial(build_kernel, gamma),
            grid=grid,
            in_specs=[whole(pts.shape), blocks(own.shape[1]), blocks(own.shape[1])],
            out_specs=[tiles, whole(u_shape.shape)],
            out_shape=[jax.ShapeDtypeStruct((CORES * n_ctr * LANES, n_pts), BF), u_shape],
            scratch_shapes=[acc] + copies(CORES) + [pltpu.VMEM((n_pts, LANES), BF)],
            compiler_params=PARAMS,
            cost_estimate=cost(4 * work * (dim + outs), 2 * work, 4 * work),
            name="build_tile",
        )(pts, own, other)

    def apply(sums, scalars, z, p, z_other, p_other, tile):
        return pl.pallas_call(
            apply_kernel,
            grid=grid,
            in_specs=[whole(sums.shape), whole(scalars.shape)] + [blocks(z.shape[1]), blocks(p.shape[1])] * 2 + [tiles],
            out_specs=whole(u_shape.shape),
            out_shape=u_shape,
            scratch_shapes=[acc] + copies(CORES) + [pltpu.VMEM((1, LANES), F32)],
            compiler_params=PARAMS,
            cost_estimate=cost(4 * work * outs, 0, 4 * work),
            name="apply_tile",
        )(sums, scalars, z, p, z_other, p_other, tile)

    def back(u, tile, half, count):
        return pl.pallas_call(
            functools.partial(back_kernel, half, count),
            grid=grid,
            in_specs=[whole(u.shape), tiles],
            out_specs=blocks(outs + RIDE),
            out_shape=jax.ShapeDtypeStruct((n_ctr, outs + RIDE, LANES), F32),
            scratch_shapes=[pltpu.VMEM((outs, n_pts), BF), pltpu.VMEM((RIDE, LANES), F32)] + copies(1),
            compiler_params=PARAMS,
            cost_estimate=cost(2 * work * outs, 0, 2 * work),
            name="back_tile",
        )(u, tile)

    def reduce_points(u, rows):
        u = jnp.sum(exchange(u, "z"), axis=0).astype(BF)
        return spread(jnp.concatenate([u, pack(rows)], 0) if rows else u, "z")

    def reduce_centres(u, tile, count):
        v = other_core(back(u, tile, 1, count))
        v = back(u, tile, 0, count) + v
        return exchange(v, "ctr")

    def local(kernel, shapes, *operands):
        return pl.pallas_call(
            functools.partial(kernel, float(total_points)),
            out_shape=[jax.ShapeDtypeStruct(shape, F32) for shape in shapes],
            compiler_params=SMALL,
            cost_estimate=cost(2 * n_ctr * outs * LANES, 0, 4 * n_ctr * outs * LANES),
            name=kernel.__name__,
        )(*operands)

    def lanes(left, right):
        return jnp.sum(left * right, axis=0)

    mine = lax.dynamic_slice_in_dim(points, lax.axis_index("ctr") * share, share, 0)
    pts = spread(mine, "z").reshape(n_pts, dim)
    p0 = direction.T
    p0_high = lax.reduce_precision(p0, 8, 7)
    parts = [centres, p0_high.astype(BF), (p0 - p0_high).astype(BF)]
    own = spread(jnp.concatenate(parts, 0), "ctr")
    other = other_core(own)

    tile, u0 = build(pts, own, other)
    z0 = precondition(factor, residual)
    u0 = reduce_points(u0, [lanes(residual.T, z0.T), lanes(p0, p0)])
    v0 = reduce_centres(u0, tile, 2)
    r1, scalars = local(first_kernel, [p0.shape, (RIDE, LANES)], v0, p0, residual.T)
    z1 = precondition(factor, r1.T).T
    zeros = [jnp.zeros((LANES,), F32)] * (RIDE - 3)
    block = jnp.stack([lanes(r1, z1), lanes(z1, z1), lanes(z1, p0)] + zeros)
    block = block + other_core(block)
    own_z = spread(jnp.concatenate([z1, block], 0), "ctr")
    other_z = other_core(own_z)
    sums = spread(jnp.sum(own_z[:, outs:], axis=0), "z")
    u1 = apply(sums, scalars, own_z, own, other_z, other, tile)
    u1 = reduce_points(u1, [])
    v1 = reduce_centres(u1, tile, 0)
    x2, r2 = local(last_kernel, [p0.shape, p0.shape], v1, sums, scalars, z1, p0, r1, solution.T)
    return x2.T, r2.T


def solution(mesh):
    shape = (mesh.shape["pt"] // CORES, CORES, mesh.shape["ctr"])
    fine = Mesh(mesh.devices.reshape(shape), ("z", "core", "ctr"))
    rows = P(("z", "core", "ctr"), None)
    return jax.shard_map(
        body,
        mesh=fine,
        in_specs=(P(("z", "core"), None),) + (rows,) * 5,
        out_specs=(rows, rows),
        check_vma=False,
    )
```

```python
import functools
import math

import jax
import jax.numpy as jnp
from jax import lax
from jax.experimental import pallas as pl
from jax.experimental.pallas import tpu as pltpu
from jax.sharding import Mesh, PartitionSpec as P

GAMMA_SCALE = 0.8
RIDGE = 64.0
CORES = 2
LANES = 128
GROUP = 2
MERGE = 2
ROWS = 16
RIDE = 8
BF = jnp.bfloat16
F32 = jnp.float32
SMALL = pltpu.CompilerParams(vmem_limit_bytes=8 * 1024 * 1024)
PARAMS = pltpu.CompilerParams(vmem_limit_bytes=52 * 1024 * 1024)


def precondition(factor, resid):
    lower = lax.linalg.triangular_solve(factor, resid, left_side=True, lower=True)
    return lax.linalg.triangular_solve(factor, lower, left_side=True, lower=True, transpose_a=True)


def exchange(blocks, axes):
    return lax.all_to_all(blocks, axes, 0, 0, tiled=True)


def spread(block, axes):
    count = lax.axis_size(axes)
    return exchange(jnp.broadcast_to(block[None], (count,) + block.shape), axes)


def other_core(block):
    return lax.ppermute(block, "core", [(0, 1), (1, 0)])


def pack(rows):
    pieces = []
    for row in rows:
        for _ in range(3):
            piece = lax.reduce_precision(row, 8, 7)
            pieces.append(piece)
            row = row - piece
    pieces += [jnp.zeros_like(pieces[0])] * (ROWS - len(pieces))
    return jnp.stack(pieces).astype(BF)


def chunks_of(total):
    half = total.shape[0] // 2
    return [
        total[part * half : (part + 1) * half, at : at + LANES]
        for at in range(0, total.shape[1], LANES)
        for part in range(2)
    ]


def add_up(step, part, u_ref, acc):
    @pl.when(step == 0)
    def _():
        acc[...] = part

    @pl.when(step > 0)
    def _():
        acc[...] += part

    @pl.when(step == pl.num_programs(0) - 1)
    def _():
        for at, piece in enumerate(chunks_of(acc[...])):
            u_ref[at] = piece


def rows_at(step):
    rows = GROUP * LANES
    return pl.ds(pl.multiple_of(step * rows, rows), rows)


def tile_copy(source, target, sems, step):
    rows = rows_at(step)
    return pltpu.make_async_copy(source.at[rows], target.at[rows], sems.at[step])


def fetch(steps, order, tile_ref, buf, sems):
    @pl.when(pl.program_id(0) == 0)
    def _():
        for at in order:
            tile_copy(tile_ref, buf, sems, at).start()

    for step in steps:
        tile_copy(tile_ref, buf, sems, step).wait()
    return [buf[rows_at(step)] for step in steps]


def gap_columns(rows, place):
    wide = rows.astype(F32)
    left = 0.5 * (rows.shape[1] - jnp.sum(wide * wide, axis=1, keepdims=True))
    lane = lax.broadcasted_iota(jnp.int32, (rows.shape[0], LANES), 1)
    columns = jnp.where(lane < 6, 1.0, 0.0)
    for k in range(3):
        piece = left.astype(BF).astype(F32)
        columns = jnp.where(lane == place + k, piece, columns)
        left = left - piece
    return columns.astype(BF)


def start_kernel(cen_ref, p_ref, out_ref):
    dim, outs = cen_ref.shape[0], p_ref.shape[0]
    high = p_ref[...].astype(BF)
    low = (p_ref[...] - high.astype(F32)).astype(BF)
    for k in range(out_ref.shape[0]):
        out_ref[k, :dim] = cen_ref[...]
        out_ref[k, dim : dim + outs] = high
        out_ref[k, dim + outs :] = low


def build_kernel(gamma, pts_ref, own_ref, other_ref, tile_ref, u_ref, acc, buf, sems, side):
    step = pl.program_id(0)
    steps = pl.num_programs(0)
    outs = acc.shape[0]

    @pl.when(step == 0)
    def _():
        side[...] = gap_columns(pts_ref[...], 3)

    pts = jnp.concatenate([pts_ref[...], side[...]], axis=1)
    part = None
    for blk_ref, place in ((own_ref, step), (other_ref, step + steps)):
        cen = jnp.concatenate([blk_ref[g, :LANES] for g in range(GROUP)], axis=0)
        vec = jnp.concatenate([blk_ref[g, LANES : LANES + outs] for g in range(GROUP)], axis=1)
        cen = jnp.concatenate([cen, gap_columns(cen, 0)], axis=1)
        cross = lax.dot_general(cen, pts, (((1,), (1,)), ((), ())), preferred_element_type=F32)
        tile = jnp.exp2((2.0 * gamma * math.log2(math.e)) * cross).astype(BF)
        buf[rows_at(place)] = tile
        tile_copy(buf, tile_ref, sems, place).start()
        term = jnp.dot(vec, tile, preferred_element_type=F32)
        part = term if part is None else part + term
    add_up(step, part, u_ref, acc)

    @pl.when(step == steps - 1)
    def _():
        for at in range(sems.shape[0]):
            tile_copy(buf, tile_ref, sems, at).wait()


def apply_kernel(sums_ref, scalars_ref, z_ref, p_ref, z_other_ref, p_other_ref, tile_ref, u_ref, acc, buf, sems, beta):
    step = pl.program_id(0)
    outs = acc.shape[0]
    count = sems.shape[0] // (2 * MERGE)

    def groups(at):
        return [MERGE * first + m for first in (at, at + count) for m in range(MERGE)]

    order = [group for at in range(count) for group in groups(at)]
    tiles = fetch(groups(step), order, tile_ref, buf, sems)

    @pl.when(step == 0)
    def _():
        rate = totals(sums_ref)[0:1] / scalars_ref[0:1, 0:1]
        beta[...] = jnp.broadcast_to(rate, beta.shape)

    part = None
    for tile, z, p in ((tiles[:MERGE], z_ref, p_ref), (tiles[MERGE:], z_other_ref, p_other_ref)):
        for m in range(MERGE):
            vec = []
            for g in range(m * GROUP, (m + 1) * GROUP):
                vec.append((z[g, :outs] + beta[...] * (p[g, :outs].astype(F32) + p[g, outs:].astype(F32))).astype(BF))
            term = jnp.dot(jnp.concatenate(vec, axis=1), tile[m], preferred_element_type=F32)
            part = term if part is None else part + term
    add_up(step, part, u_ref, acc)


def back_kernel(half, count, u_ref, tile_ref, v_ref, ub, ride, buf, sems):
    rows = buf.shape[0]
    outs = ub.shape[0]
    step = pl.program_id(0)
    tile = fetch([step], range(sems.shape[0]), tile_ref.at[pl.ds(half * rows, rows)], buf, sems)[0]
    half = outs // 2

    @pl.when(step == 0)
    def _():
        squares = jnp.zeros((half, LANES), F32)
        for at in range(u_ref.shape[0]):
            piece = u_ref[at, :half]
            low = (at % 2) * half
            ub[low : low + half, (at // 2) * LANES : (at // 2 + 1) * LANES] = piece
            squares += piece.astype(F32) * piece.astype(F32)
        packed = jnp.sum(u_ref[:, half:].astype(F32), axis=0) if count else None
        rows = [packed[3 * k : 3 * k + 1] + packed[3 * k + 1 : 3 * k + 2] + packed[3 * k + 2 : 3 * k + 3] for k in range(count)]
        rows.append(jnp.sum(squares, axis=0, keepdims=True))
        rows.append(jnp.zeros((RIDE - count - 1, LANES), F32))
        ride[...] = jnp.concatenate(rows, axis=0)

    v = lax.dot_general(ub[...], tile, (((1,), (1,)), ((), ())), preferred_element_type=F32)
    for g in range(GROUP):
        v_ref[g, :outs] = v[:, g * LANES : (g + 1) * LANES]
        v_ref[g, outs:] = ride[...]


def totals(sums_ref):
    return jnp.sum(jnp.sum(sums_ref[...], axis=0), axis=1, keepdims=True)


def first_kernel(points, v_ref, p_ref, r_ref, r1_ref, scalars_ref):
    outs = p_ref.shape[0]
    v = jnp.sum(v_ref[...], axis=0)
    s = jnp.sum(v[outs:], axis=1, keepdims=True)
    alpha = s[0:1] / (s[2:3] / points + RIDGE * s[1:2])
    r1_ref[...] = r_ref[...] - alpha * (v[:outs] / points + RIDGE * p_ref[...])
    rows = [jnp.broadcast_to(value, (1, LANES)) for value in (s[0:1], s[1:2], alpha)]
    scalars_ref[...] = jnp.concatenate(rows + [jnp.zeros((RIDE - 3, LANES), F32)], axis=0)


def last_kernel(points, v_ref, sums_ref, scalars_ref, z_ref, p_ref, r_ref, x_ref, x_out, r_out):
    outs = p_ref.shape[0]
    v = jnp.sum(v_ref[...], axis=0)
    uu = jnp.sum(v[outs : outs + 1], axis=1, keepdims=True)
    t = totals(sums_ref)
    rz0, pp0, alpha0 = [scalars_ref[k : k + 1, 0:1] for k in range(3)]
    beta = t[0:1] / rz0
    p1 = z_ref[...] + beta * p_ref[...]
    pp = t[1:2] + beta * (2.0 * t[2:3] + beta * pp0)
    alpha1 = t[0:1] / (uu / points + RIDGE * pp)
    x_out[...] = x_ref[...] + alpha0 * p_ref[...] + alpha1 * p1
    r_out[...] = r_ref[...] - alpha1 * (v[:outs] / points + RIDGE * p1)


def body(points, centres, factor, solution, residual, direction):
    dim = points.shape[1]
    gamma = GAMMA_SCALE / math.sqrt(dim)
    outs = direction.shape[1]
    n_z, n_ctr = lax.axis_size("z"), lax.axis_size("ctr")
    total_points = points.shape[0] * n_z * CORES
    n_pts = points.shape[0]
    share = n_pts // n_ctr
    grid = (n_ctr // GROUP,)
    u_shape = jax.ShapeDtypeStruct((2 * n_pts // LANES, outs // 2, LANES), F32)
    whole = lambda shape: pl.BlockSpec(shape, lambda i: (0,) * len(shape))
    blocks = lambda rows: pl.BlockSpec((GROUP, rows, LANES), lambda i: (i, 0, 0))
    tiles = pl.BlockSpec(memory_space=pltpu.HBM)

    def copies(halves):
        return [pltpu.VMEM((halves * n_ctr * LANES, n_pts), BF), pltpu.SemaphoreType.DMA((halves * grid[0],))]
    acc = pltpu.VMEM((outs, n_pts), F32)
    work = n_ctr * LANES * n_pts

    def cost(flops, exps, size):
        return pl.CostEstimate(flops=flops, transcendentals=exps, bytes_accessed=size)

    def build(pts, own, other):
        return pl.pallas_call(
            functools.partial(build_kernel, gamma),
            grid=grid,
            in_specs=[whole(pts.shape), blocks(own.shape[1]), blocks(own.shape[1])],
            out_specs=[tiles, whole(u_shape.shape)],
            out_shape=[jax.ShapeDtypeStruct((CORES * n_ctr * LANES, n_pts), BF), u_shape],
            scratch_shapes=[acc] + copies(CORES) + [pltpu.VMEM((n_pts, LANES), BF)],
            compiler_params=PARAMS,
            cost_estimate=cost(4 * work * (dim + outs), 2 * work, 4 * work),
            name="build_tile",
        )(pts, own, other)

    def apply(sums, scalars, z, p, z_other, p_other, tile):
        step_z = pl.BlockSpec((MERGE * GROUP, z.shape[1], LANES), lambda i: (i, 0, 0))
        step_p = pl.BlockSpec((MERGE * GROUP, 2 * outs, LANES), lambda i: (i, 1, 0))
        return pl.pallas_call(
            apply_kernel,
            grid=(grid[0] // MERGE,),
            in_specs=[whole(sums.shape), whole(scalars.shape)] + [step_z, step_p] * 2 + [tiles],
            out_specs=whole(u_shape.shape),
            out_shape=u_shape,
            scratch_shapes=[acc] + copies(CORES) + [pltpu.VMEM((1, LANES), F32)],
            compiler_params=PARAMS,
            cost_estimate=cost(4 * work * outs, 0, 4 * work),
            name="apply_tile",
        )(sums, scalars, z, p, z_other, p_other, tile)

    def back(u, tile, half, count):
        return pl.pallas_call(
            functools.partial(back_kernel, half, count),
            grid=grid,
            in_specs=[whole(u.shape), tiles],
            out_specs=blocks(outs + RIDE),
            out_shape=jax.ShapeDtypeStruct((n_ctr, outs + RIDE, LANES), F32),
            scratch_shapes=[pltpu.VMEM((outs, n_pts), BF), pltpu.VMEM((RIDE, LANES), F32)] + copies(1),
            compiler_params=PARAMS,
            cost_estimate=cost(2 * work * outs, 0, 2 * work),
            name="back_tile",
        )(u, tile)

    def reduce_points(u, rows):
        u = jnp.sum(exchange(u, "z"), axis=0).astype(BF)
        return spread(jnp.concatenate([u, pack(rows)], 0) if rows else u, "z")

    def reduce_centres(u, tile, count):
        v = other_core(back(u, tile, 1, count))
        v = back(u, tile, 0, count) + v
        return exchange(v, "ctr")

    def local(kernel, shapes, *operands):
        return pl.pallas_call(
            functools.partial(kernel, float(total_points)),
            out_shape=[jax.ShapeDtypeStruct(shape, F32) for shape in shapes],
            compiler_params=SMALL,
            cost_estimate=cost(2 * n_ctr * outs * LANES, 0, 4 * n_ctr * outs * LANES),
            name=kernel.__name__,
        )(*operands)

    def lanes(left, right):
        return jnp.sum(left * right, axis=0)

    mine = lax.dynamic_slice_in_dim(points, lax.axis_index("ctr") * share, share, 0)
    pts = spread(mine, "z").reshape(n_pts, dim)
    p0 = direction.T
    parts = pl.pallas_call(
        start_kernel,
        out_shape=jax.ShapeDtypeStruct((n_ctr, LANES + 2 * outs, dim), BF),
        compiler_params=SMALL,
        name="start_kernel",
    )(centres, p0)
    own = exchange(parts, "ctr")
    other = other_core(own)

    tile, u0 = build(pts, own, other)
    z0 = precondition(factor, residual)
    u0 = reduce_points(u0, [lanes(residual.T, z0.T), lanes(p0, p0)])
    v0 = reduce_centres(u0, tile, 2)
    r1, scalars = local(first_kernel, [p0.shape, (RIDE, LANES)], v0, p0, residual.T)
    z1 = precondition(factor, r1.T).T
    zeros = [jnp.zeros((LANES,), F32)] * (RIDE - 3)
    block = jnp.stack([lanes(r1, z1), lanes(z1, z1), lanes(z1, p0)] + zeros)
    block = block + other_core(block)
    own_z = spread(jnp.concatenate([z1, block], 0), "ctr")
    other_z = other_core(own_z)
    sums = spread(jnp.sum(own_z[:, outs:], axis=0), "z")
    u1 = apply(sums, scalars, own_z, own, other_z, other, tile)
    u1 = reduce_points(u1, [])
    v1 = reduce_centres(u1, tile, 0)
    x2, r2 = local(last_kernel, [p0.shape, p0.shape], v1, sums, scalars, z1, p0, r1, solution.T)
    return x2.T, r2.T


def solution(mesh):
    shape = (mesh.shape["pt"] // CORES, CORES, mesh.shape["ctr"])
    fine = Mesh(mesh.devices.reshape(shape), ("z", "core", "ctr"))
    rows = P(("z", "core", "ctr"), None)
    return jax.shard_map(
        body,
        mesh=fine,
        in_specs=(P(("z", "core"), None),) + (rows,) * 5,
        out_specs=(rows, rows),
        check_vma=False,
    )
```

```python
import functools
import math

import jax
import jax.numpy as jnp
from jax import lax
from jax.experimental import pallas as pl
from jax.experimental.pallas import tpu as pltpu
from jax.sharding import Mesh, PartitionSpec as P

GAMMA_SCALE = 0.8
RIDGE = 64.0
CORES = 2
LANES = 128
GROUP = 2
MERGE = 2
ROWS = 16
RIDE = 8
BF = jnp.bfloat16
F32 = jnp.float32
SMALL = pltpu.CompilerParams(vmem_limit_bytes=8 * 1024 * 1024)
PARAMS = pltpu.CompilerParams(vmem_limit_bytes=50 * 1024 * 1024)


def precondition(factor, resid):
    lower = lax.linalg.triangular_solve(factor, resid, left_side=True, lower=True)
    return lax.linalg.triangular_solve(factor, lower, left_side=True, lower=True, transpose_a=True)


def exchange(blocks, axes):
    return lax.all_to_all(blocks, axes, 0, 0, tiled=True)


def spread(block, axes):
    count = lax.axis_size(axes)
    return exchange(jnp.broadcast_to(block[None], (count,) + block.shape), axes)


def other_core(block):
    return lax.ppermute(block, "core", [(0, 1), (1, 0)])


def pack(rows):
    pieces = []
    for row in rows:
        for _ in range(3):
            piece = lax.reduce_precision(row, 8, 7)
            pieces.append(piece)
            row = row - piece
    pieces += [jnp.zeros_like(pieces[0])] * (ROWS - len(pieces))
    return jnp.stack(pieces).astype(BF)


def chunks_of(total):
    half = total.shape[0] // 2
    return [
        total[part * half : (part + 1) * half, at : at + LANES]
        for at in range(0, total.shape[1], LANES)
        for part in range(2)
    ]


def add_up(step, part, u_ref, acc):
    @pl.when(step == 0)
    def _():
        acc[...] = part

    @pl.when(step > 0)
    def _():
        acc[...] += part

    @pl.when(step == pl.num_programs(0) - 1)
    def _():
        for at, piece in enumerate(chunks_of(acc[...])):
            u_ref[at] = piece


def rows_at(step):
    rows = GROUP * LANES
    return pl.ds(pl.multiple_of(step * rows, rows), rows)


def tile_copy(source, target, sems, step):
    rows = rows_at(step)
    return pltpu.make_async_copy(source.at[rows], target.at[rows], sems.at[step])


def fetch(steps, order, tile_ref, buf, sems):
    @pl.when(pl.program_id(0) == 0)
    def _():
        for at in order:
            tile_copy(tile_ref, buf, sems, at).start()

    for step in steps:
        tile_copy(tile_ref, buf, sems, step).wait()
    return [buf[rows_at(step)] for step in steps]


def gap_columns(rows, place):
    wide = rows.astype(F32)
    left = 0.5 * (rows.shape[1] - jnp.sum(wide * wide, axis=1, keepdims=True))
    lane = lax.broadcasted_iota(jnp.int32, (rows.shape[0], LANES), 1)
    columns = jnp.where(lane < 6, 1.0, 0.0)
    for k in range(3):
        piece = left.astype(BF).astype(F32)
        columns = jnp.where(lane == place + k, piece, columns)
        left = left - piece
    return columns.astype(BF)


def start_kernel(cen_ref, p_ref, out_ref):
    dim, outs = cen_ref.shape[0], p_ref.shape[0]
    high = p_ref[...].astype(BF)
    low = (p_ref[...] - high.astype(F32)).astype(BF)
    for k in range(out_ref.shape[0]):
        out_ref[k, :dim] = cen_ref[...]
        out_ref[k, dim : dim + outs] = high
        out_ref[k, dim + outs :] = low


def build_kernel(gamma, pts_ref, own_ref, other_ref, tile_ref, u_ref, acc, buf, sems, side):
    step = pl.program_id(0)
    steps = pl.num_programs(0)
    outs = acc.shape[0]

    @pl.when(step == 0)
    def _():
        side[...] = gap_columns(pts_ref[...], 3)

    pts = jnp.concatenate([pts_ref[...], side[...]], axis=1)
    part = None
    for blk_ref, place in ((own_ref, step), (other_ref, step + steps)):
        cen = jnp.concatenate([blk_ref[g, :LANES] for g in range(GROUP)], axis=0)
        vec = jnp.concatenate([blk_ref[g, LANES : LANES + outs] for g in range(GROUP)], axis=1)
        cen = jnp.concatenate([cen, gap_columns(cen, 0)], axis=1)
        cross = lax.dot_general(cen, pts, (((1,), (1,)), ((), ())), preferred_element_type=F32)
        tile = jnp.exp2((2.0 * gamma * math.log2(math.e)) * cross).astype(BF)
        buf[rows_at(place)] = tile
        tile_copy(buf, tile_ref, sems, place).start()
        term = jnp.dot(vec, tile, preferred_element_type=F32)
        part = term if part is None else part + term
    add_up(step, part, u_ref, acc)

    @pl.when(step == steps - 1)
    def _():
        for at in range(sems.shape[0]):
            tile_copy(buf, tile_ref, sems, at).wait()


def apply_kernel(sums_ref, scalars_ref, z_ref, p_ref, z_other_ref, p_other_ref, tile_ref, u_ref, acc, buf, sems, beta):
    step = pl.program_id(0)
    outs = acc.shape[0]
    count = sems.shape[0] // (2 * MERGE)

    def groups(at):
        return [MERGE * first + m for first in (at, at + count) for m in range(MERGE)]

    order = [group for at in range(count) for group in groups(at)]
    tiles = fetch(groups(step), order, tile_ref, buf, sems)

    @pl.when(step == 0)
    def _():
        rate = totals(sums_ref)[0:1] / scalars_ref[0:1, 0:1]
        beta[...] = jnp.broadcast_to(rate, beta.shape)

    part = None
    for tile, z, p in ((tiles[:MERGE], z_ref, p_ref), (tiles[MERGE:], z_other_ref, p_other_ref)):
        for m in range(MERGE):
            vec = []
            for g in range(m * GROUP, (m + 1) * GROUP):
                vec.append((z[g, :outs] + beta[...] * (p[g, :outs].astype(F32) + p[g, outs:].astype(F32))).astype(BF))
            term = jnp.dot(jnp.concatenate(vec, axis=1), tile[m], preferred_element_type=F32)
            part = term if part is None else part + term
    add_up(step, part, u_ref, acc)


def back_kernel(half, count, u_ref, tile_ref, v_ref, ub, ride, buf, sems):
    rows = buf.shape[0]
    outs = ub.shape[0]
    step = pl.program_id(0)
    mine = [MERGE * step + m for m in range(MERGE)]
    tiles = fetch(mine, range(sems.shape[0]), tile_ref.at[pl.ds(half * rows, rows)], buf, sems)
    half = outs // 2

    @pl.when(step == 0)
    def _():
        squares = jnp.zeros((half, LANES), F32)
        for at in range(u_ref.shape[0]):
            piece = u_ref[at, :half]
            low = (at % 2) * half
            ub[low : low + half, (at // 2) * LANES : (at // 2 + 1) * LANES] = piece
            squares += piece.astype(F32) * piece.astype(F32)
        packed = jnp.sum(u_ref[:, half:].astype(F32), axis=0) if count else None
        rows = [packed[3 * k : 3 * k + 1] + packed[3 * k + 1 : 3 * k + 2] + packed[3 * k + 2 : 3 * k + 3] for k in range(count)]
        rows.append(jnp.sum(squares, axis=0, keepdims=True))
        rows.append(jnp.zeros((RIDE - count - 1, LANES), F32))
        ride[...] = jnp.concatenate(rows, axis=0)

    for m, tile in enumerate(tiles):
        v = lax.dot_general(ub[...], tile, (((1,), (1,)), ((), ())), preferred_element_type=F32)
        for g in range(GROUP):
            v_ref[m * GROUP + g, :outs] = v[:, g * LANES : (g + 1) * LANES]
            v_ref[m * GROUP + g, outs:] = ride[...]


def totals(sums_ref):
    return jnp.sum(jnp.sum(sums_ref[...], axis=0), axis=1, keepdims=True)


def first_kernel(points, v_ref, p_ref, r_ref, r1_ref, scalars_ref):
    outs = p_ref.shape[0]
    v = jnp.sum(v_ref[...], axis=0)
    s = jnp.sum(v[outs:], axis=1, keepdims=True)
    alpha = s[0:1] / (s[2:3] / points + RIDGE * s[1:2])
    r1_ref[...] = r_ref[...] - alpha * (v[:outs] / points + RIDGE * p_ref[...])
    rows = [jnp.broadcast_to(value, (1, LANES)) for value in (s[0:1], s[1:2], alpha)]
    scalars_ref[...] = jnp.concatenate(rows + [jnp.zeros((RIDE - 3, LANES), F32)], axis=0)


def last_kernel(points, v_ref, sums_ref, scalars_ref, z_ref, p_ref, r_ref, x_ref, x_out, r_out):
    outs = p_ref.shape[0]
    v = jnp.sum(v_ref[...], axis=0)
    uu = jnp.sum(v[outs : outs + 1], axis=1, keepdims=True)
    t = totals(sums_ref)
    rz0, pp0, alpha0 = [scalars_ref[k : k + 1, 0:1] for k in range(3)]
    beta = t[0:1] / rz0
    p1 = z_ref[...] + beta * p_ref[...]
    pp = t[1:2] + beta * (2.0 * t[2:3] + beta * pp0)
    alpha1 = t[0:1] / (uu / points + RIDGE * pp)
    x_out[...] = x_ref[...] + alpha0 * p_ref[...] + alpha1 * p1
    r_out[...] = r_ref[...] - alpha1 * (v[:outs] / points + RIDGE * p1)


def body(points, centres, factor, solution, residual, direction):
    dim = points.shape[1]
    gamma = GAMMA_SCALE / math.sqrt(dim)
    outs = direction.shape[1]
    n_z, n_ctr = lax.axis_size("z"), lax.axis_size("ctr")
    total_points = points.shape[0] * n_z * CORES
    n_pts = points.shape[0]
    share = n_pts // n_ctr
    grid = (n_ctr // GROUP,)
    u_shape = jax.ShapeDtypeStruct((2 * n_pts // LANES, outs // 2, LANES), F32)
    whole = lambda shape: pl.BlockSpec(shape, lambda i: (0,) * len(shape))
    blocks = lambda rows: pl.BlockSpec((GROUP, rows, LANES), lambda i: (i, 0, 0))
    tiles = pl.BlockSpec(memory_space=pltpu.HBM)

    def copies(halves):
        return [pltpu.VMEM((halves * n_ctr * LANES, n_pts), BF), pltpu.SemaphoreType.DMA((halves * grid[0],))]
    acc = pltpu.VMEM((outs, n_pts), F32)
    work = n_ctr * LANES * n_pts

    def cost(flops, exps, size):
        return pl.CostEstimate(flops=flops, transcendentals=exps, bytes_accessed=size)

    def build(pts, own, other):
        return pl.pallas_call(
            functools.partial(build_kernel, gamma),
            grid=grid,
            in_specs=[whole(pts.shape), blocks(own.shape[1]), blocks(own.shape[1])],
            out_specs=[tiles, whole(u_shape.shape)],
            out_shape=[jax.ShapeDtypeStruct((CORES * n_ctr * LANES, n_pts), BF), u_shape],
            scratch_shapes=[acc] + copies(CORES) + [pltpu.VMEM((n_pts, LANES), BF)],
            compiler_params=PARAMS,
            cost_estimate=cost(4 * work * (dim + outs), 2 * work, 4 * work),
            name="build_tile",
        )(pts, own, other)

    def apply(sums, scalars, z, p, z_other, p_other, tile):
        step_z = pl.BlockSpec((MERGE * GROUP, z.shape[1], LANES), lambda i: (i, 0, 0))
        step_p = pl.BlockSpec((MERGE * GROUP, 2 * outs, LANES), lambda i: (i, 1, 0))
        return pl.pallas_call(
            apply_kernel,
            grid=(grid[0] // MERGE,),
            in_specs=[whole(sums.shape), whole(scalars.shape)] + [step_z, step_p] * 2 + [tiles],
            out_specs=whole(u_shape.shape),
            out_shape=u_shape,
            scratch_shapes=[acc] + copies(CORES) + [pltpu.VMEM((1, LANES), F32)],
            compiler_params=PARAMS,
            cost_estimate=cost(4 * work * outs, 0, 4 * work),
            name="apply_tile",
        )(sums, scalars, z, p, z_other, p_other, tile)

    def back(u, tile, half, count):
        return pl.pallas_call(
            functools.partial(back_kernel, half, count),
            grid=(grid[0] // MERGE,),
            in_specs=[whole(u.shape), tiles],
            out_specs=pl.BlockSpec((MERGE * GROUP, outs + RIDE, LANES), lambda i: (i, 0, 0)),
            out_shape=jax.ShapeDtypeStruct((n_ctr, outs + RIDE, LANES), F32),
            scratch_shapes=[pltpu.VMEM((outs, n_pts), BF), pltpu.VMEM((RIDE, LANES), F32)] + copies(1),
            compiler_params=PARAMS,
            cost_estimate=cost(2 * work * outs, 0, 2 * work),
            name="back_tile",
        )(u, tile)

    def reduce_points(u, rows):
        u = jnp.sum(exchange(u, "z"), axis=0).astype(BF)
        return spread(jnp.concatenate([u, pack(rows)], 0) if rows else u, "z")

    def reduce_centres(u, tile, count):
        v = other_core(back(u, tile, 1, count))
        v = back(u, tile, 0, count) + v
        return exchange(v, "ctr")

    def local(kernel, shapes, *operands):
        return pl.pallas_call(
            functools.partial(kernel, float(total_points)),
            out_shape=[jax.ShapeDtypeStruct(shape, F32) for shape in shapes],
            compiler_params=SMALL,
            cost_estimate=cost(2 * n_ctr * outs * LANES, 0, 4 * n_ctr * outs * LANES),
            name=kernel.__name__,
        )(*operands)

    def lanes(left, right):
        return jnp.sum(left * right, axis=0)

    mine = lax.dynamic_slice_in_dim(points, lax.axis_index("ctr") * share, share, 0)
    pts = spread(mine, "z").reshape(n_pts, dim)
    p0 = direction.T
    parts = pl.pallas_call(
        start_kernel,
        out_shape=jax.ShapeDtypeStruct((n_ctr, LANES + 2 * outs, dim), BF),
        compiler_params=SMALL,
        name="start_kernel",
    )(centres, p0)
    own = exchange(parts, "ctr")
    other = other_core(own)

    tile, u0 = build(pts, own, other)
    z0 = precondition(factor, residual)
    u0 = reduce_points(u0, [lanes(residual.T, z0.T), lanes(p0, p0)])
    v0 = reduce_centres(u0, tile, 2)
    r1, scalars = local(first_kernel, [p0.shape, (RIDE, LANES)], v0, p0, residual.T)
    z1 = precondition(factor, r1.T).T
    zeros = [jnp.zeros((LANES,), F32)] * (RIDE - 3)
    block = jnp.stack([lanes(r1, z1), lanes(z1, z1), lanes(z1, p0)] + zeros)
    block = block + other_core(block)
    own_z = spread(jnp.concatenate([z1, block], 0), "ctr")
    other_z = other_core(own_z)
    sums = spread(jnp.sum(own_z[:, outs:], axis=0), "z")
    u1 = apply(sums, scalars, own_z, own, other_z, other, tile)
    u1 = reduce_points(u1, [])
    v1 = reduce_centres(u1, tile, 0)
    x2, r2 = local(last_kernel, [p0.shape, p0.shape], v1, sums, scalars, z1, p0, r1, solution.T)
    return x2.T, r2.T


def solution(mesh):
    shape = (mesh.shape["pt"] // CORES, CORES, mesh.shape["ctr"])
    fine = Mesh(mesh.devices.reshape(shape), ("z", "core", "ctr"))
    rows = P(("z", "core", "ctr"), None)
    return jax.shard_map(
        body,
        mesh=fine,
        in_specs=(P(("z", "core"), None),) + (rows,) * 5,
        out_specs=(rows, rows),
        check_vma=False,
    )
```

```python
import functools
import math

import jax
import jax.numpy as jnp
from jax import lax
from jax.experimental import pallas as pl
from jax.experimental.pallas import tpu as pltpu
from jax.sharding import Mesh, PartitionSpec as P

GAMMA_SCALE = 0.8
RIDGE = 64.0
CORES = 2
LANES = 128
GROUP = 2
MERGE = 2
ROWS = 16
RIDE = 8
BF = jnp.bfloat16
F32 = jnp.float32
SMALL = pltpu.CompilerParams(vmem_limit_bytes=8 * 1024 * 1024)
PARAMS = pltpu.CompilerParams(vmem_limit_bytes=50 * 1024 * 1024)


def precondition(factor, resid):
    lower = lax.linalg.triangular_solve(factor, resid, left_side=True, lower=True)
    return lax.linalg.triangular_solve(factor, lower, left_side=True, lower=True, transpose_a=True)


def exchange(blocks, axes):
    return lax.all_to_all(blocks, axes, 0, 0, tiled=True)


def spread(block, axes):
    count = lax.axis_size(axes)
    return exchange(jnp.broadcast_to(block[None], (count,) + block.shape), axes)


def other_core(block):
    return lax.ppermute(block, "core", [(0, 1), (1, 0)])


def pack(rows):
    pieces = []
    for row in rows:
        for _ in range(3):
            piece = lax.reduce_precision(row, 8, 7)
            pieces.append(piece)
            row = row - piece
    pieces += [jnp.zeros_like(pieces[0])] * (ROWS - len(pieces))
    return jnp.stack(pieces).astype(BF)


def chunks_of(total):
    half = total.shape[0] // 2
    return [
        total[part * half : (part + 1) * half, at : at + LANES]
        for at in range(0, total.shape[1], LANES)
        for part in range(2)
    ]


def add_up(step, part, u_ref, acc):
    @pl.when(step == 0)
    def _():
        acc[...] = part

    @pl.when(step > 0)
    def _():
        acc[...] += part

    @pl.when(step == pl.num_programs(0) - 1)
    def _():
        for at, piece in enumerate(chunks_of(acc[...])):
            u_ref[at] = piece


def rows_at(step):
    rows = GROUP * LANES
    return pl.ds(pl.multiple_of(step * rows, rows), rows)


def tile_copy(source, target, sems, step):
    rows = rows_at(step)
    return pltpu.make_async_copy(source.at[rows], target.at[rows], sems.at[step])


def fetch(steps, order, tile_ref, buf, sems):
    @pl.when(pl.program_id(0) == 0)
    def _():
        for at in order:
            tile_copy(tile_ref, buf, sems, at).start()

    for step in steps:
        tile_copy(tile_ref, buf, sems, step).wait()
    return [buf[rows_at(step)] for step in steps]


def gap_columns(rows, place):
    wide = rows.astype(F32)
    left = 0.5 * (rows.shape[1] - jnp.sum(wide * wide, axis=1, keepdims=True))
    lane = lax.broadcasted_iota(jnp.int32, (rows.shape[0], LANES), 1)
    columns = jnp.where(lane < 6, 1.0, 0.0)
    for k in range(3):
        piece = left.astype(BF).astype(F32)
        columns = jnp.where(lane == place + k, piece, columns)
        left = left - piece
    return columns.astype(BF)


def start_kernel(cen_hbm, p_hbm, out_ref, cen_ref, p_ref, sems):
    dim, outs = cen_ref.shape[0], p_ref.shape[0]
    reads = [pltpu.make_async_copy(cen_hbm, cen_ref, sems.at[0]), pltpu.make_async_copy(p_hbm, p_ref, sems.at[1])]
    for read in reads:
        read.start()
    for read in reads:
        read.wait()
    high = p_ref[...].astype(BF)
    low = (p_ref[...] - high.astype(F32)).astype(BF)
    for k in range(out_ref.shape[0]):
        out_ref[k, :dim] = cen_ref[...]
        out_ref[k, dim : dim + outs] = high
        out_ref[k, dim + outs :] = low


def build_kernel(gamma, pts_ref, own_ref, other_ref, tile_ref, u_ref, acc, buf, sems, side):
    step = pl.program_id(0)
    steps = pl.num_programs(0)
    outs = acc.shape[0]

    @pl.when(step == 0)
    def _():
        side[...] = gap_columns(pts_ref[...], 3)

    pts = jnp.concatenate([pts_ref[...], side[...]], axis=1)
    part = None
    for blk_ref, first in ((own_ref, step), (other_ref, step + steps)):
        for m in range(MERGE):
            blks = [blk_ref[g] for g in range(m * GROUP, (m + 1) * GROUP)]
            place = MERGE * first + m
            cen = jnp.concatenate([blk[:LANES] for blk in blks], axis=0)
            vec = jnp.concatenate([blk[LANES : LANES + outs] for blk in blks], axis=1)
            cen = jnp.concatenate([cen, gap_columns(cen, 0)], axis=1)
            cross = lax.dot_general(cen, pts, (((1,), (1,)), ((), ())), preferred_element_type=F32)
            tile = jnp.exp2((2.0 * gamma * math.log2(math.e)) * cross).astype(BF)
            buf[rows_at(place)] = tile
            tile_copy(buf, tile_ref, sems, place).start()
            term = jnp.dot(vec, tile, preferred_element_type=F32)
            part = term if part is None else part + term
    add_up(step, part, u_ref, acc)

    @pl.when(step == steps - 1)
    def _():
        for at in range(sems.shape[0]):
            tile_copy(buf, tile_ref, sems, at).wait()


def apply_kernel(sums_ref, scalars_ref, z_ref, p_ref, z_other_ref, p_other_ref, tile_ref, u_ref, acc, buf, sems, beta):
    step = pl.program_id(0)
    outs = acc.shape[0]
    count = sems.shape[0] // (2 * MERGE)

    def groups(at):
        return [MERGE * first + m for first in (at, at + count) for m in range(MERGE)]

    order = [group for at in range(count) for group in groups(at)]
    tiles = fetch(groups(step), order, tile_ref, buf, sems)

    @pl.when(step == 0)
    def _():
        rate = totals(sums_ref)[0:1] / scalars_ref[0:1, 0:1]
        beta[...] = jnp.broadcast_to(rate, beta.shape)

    part = None
    for tile, z, p in ((tiles[:MERGE], z_ref, p_ref), (tiles[MERGE:], z_other_ref, p_other_ref)):
        for m in range(MERGE):
            vec = []
            for g in range(m * GROUP, (m + 1) * GROUP):
                vec.append((z[g, :outs] + beta[...] * (p[g, :outs].astype(F32) + p[g, outs:].astype(F32))).astype(BF))
            term = jnp.dot(jnp.concatenate(vec, axis=1), tile[m], preferred_element_type=F32)
            part = term if part is None else part + term
    add_up(step, part, u_ref, acc)


def back_kernel(half, count, u_ref, tile_ref, v_ref, ub, ride, buf, sems):
    rows = buf.shape[0]
    outs = ub.shape[0]
    step = pl.program_id(0)
    mine = [MERGE * step + m for m in range(MERGE)]
    tiles = fetch(mine, range(sems.shape[0]), tile_ref.at[pl.ds(half * rows, rows)], buf, sems)
    half = outs // 2

    @pl.when(step == 0)
    def _():
        squares = jnp.zeros((half, LANES), F32)
        for at in range(u_ref.shape[0]):
            piece = u_ref[at, :half]
            low = (at % 2) * half
            ub[low : low + half, (at // 2) * LANES : (at // 2 + 1) * LANES] = piece
            squares += piece.astype(F32) * piece.astype(F32)
        packed = jnp.sum(u_ref[:, half:].astype(F32), axis=0) if count else None
        rows = [packed[3 * k : 3 * k + 1] + packed[3 * k + 1 : 3 * k + 2] + packed[3 * k + 2 : 3 * k + 3] for k in range(count)]
        rows.append(jnp.sum(squares, axis=0, keepdims=True))
        rows.append(jnp.zeros((RIDE - count - 1, LANES), F32))
        ride[...] = jnp.concatenate(rows, axis=0)

    for m, tile in enumerate(tiles):
        v = lax.dot_general(ub[...], tile, (((1,), (1,)), ((), ())), preferred_element_type=F32)
        for g in range(GROUP):
            v_ref[m * GROUP + g, :outs] = v[:, g * LANES : (g + 1) * LANES]
            v_ref[m * GROUP + g, outs:] = ride[...]


def totals(sums_ref):
    return jnp.sum(jnp.sum(sums_ref[...], axis=0), axis=1, keepdims=True)


def first_kernel(points, v_ref, p_ref, r_ref, r1_ref, scalars_ref):
    outs = p_ref.shape[0]
    v = jnp.sum(v_ref[...], axis=0)
    s = jnp.sum(v[outs:], axis=1, keepdims=True)
    alpha = s[0:1] / (s[2:3] / points + RIDGE * s[1:2])
    r1_ref[...] = r_ref[...] - alpha * (v[:outs] / points + RIDGE * p_ref[...])
    rows = [jnp.broadcast_to(value, (1, LANES)) for value in (s[0:1], s[1:2], alpha)]
    scalars_ref[...] = jnp.concatenate(rows + [jnp.zeros((RIDE - 3, LANES), F32)], axis=0)


def last_kernel(points, v_ref, sums_ref, scalars_ref, z_ref, p_ref, r_ref, x_ref, x_out, r_out):
    outs = p_ref.shape[0]
    v = jnp.sum(v_ref[...], axis=0)
    uu = jnp.sum(v[outs : outs + 1], axis=1, keepdims=True)
    t = totals(sums_ref)
    rz0, pp0, alpha0 = [scalars_ref[k : k + 1, 0:1] for k in range(3)]
    beta = t[0:1] / rz0
    p1 = z_ref[...] + beta * p_ref[...]
    pp = t[1:2] + beta * (2.0 * t[2:3] + beta * pp0)
    alpha1 = t[0:1] / (uu / points + RIDGE * pp)
    x_out[...] = x_ref[...] + alpha0 * p_ref[...] + alpha1 * p1
    r_out[...] = r_ref[...] - alpha1 * (v[:outs] / points + RIDGE * p1)


def body(points, centres, factor, solution, residual, direction):
    dim = points.shape[1]
    gamma = GAMMA_SCALE / math.sqrt(dim)
    outs = direction.shape[1]
    n_z, n_ctr = lax.axis_size("z"), lax.axis_size("ctr")
    total_points = points.shape[0] * n_z * CORES
    n_pts = points.shape[0]
    share = n_pts // n_ctr
    grid = (n_ctr // GROUP,)
    u_shape = jax.ShapeDtypeStruct((2 * n_pts // LANES, outs // 2, LANES), F32)
    whole = lambda shape: pl.BlockSpec(shape, lambda i: (0,) * len(shape))
    tiles = pl.BlockSpec(memory_space=pltpu.HBM)

    def copies(halves):
        return [pltpu.VMEM((halves * n_ctr * LANES, n_pts), BF), pltpu.SemaphoreType.DMA((halves * grid[0],))]
    acc = pltpu.VMEM((outs, n_pts), F32)
    work = n_ctr * LANES * n_pts

    def cost(flops, exps, size):
        return pl.CostEstimate(flops=flops, transcendentals=exps, bytes_accessed=size)

    def build(pts, own, other):
        return pl.pallas_call(
            functools.partial(build_kernel, gamma),
            grid=(grid[0] // MERGE,),
            in_specs=[whole(pts.shape)] + [pl.BlockSpec((MERGE * GROUP, own.shape[1], LANES), lambda i: (i, 0, 0))] * 2,
            out_specs=[tiles, whole(u_shape.shape)],
            out_shape=[jax.ShapeDtypeStruct((CORES * n_ctr * LANES, n_pts), BF), u_shape],
            scratch_shapes=[acc] + copies(CORES) + [pltpu.VMEM((n_pts, LANES), BF)],
            compiler_params=PARAMS,
            cost_estimate=cost(4 * work * (dim + outs), 2 * work, 4 * work),
            name="build_tile",
        )(pts, own, other)

    def apply(sums, scalars, z, p, z_other, p_other, tile):
        step_z = pl.BlockSpec((MERGE * GROUP, z.shape[1], LANES), lambda i: (i, 0, 0))
        step_p = pl.BlockSpec((MERGE * GROUP, 2 * outs, LANES), lambda i: (i, 1, 0))
        return pl.pallas_call(
            apply_kernel,
            grid=(grid[0] // MERGE,),
            in_specs=[whole(sums.shape), whole(scalars.shape)] + [step_z, step_p] * 2 + [tiles],
            out_specs=whole(u_shape.shape),
            out_shape=u_shape,
            scratch_shapes=[acc] + copies(CORES) + [pltpu.VMEM((1, LANES), F32)],
            compiler_params=PARAMS,
            cost_estimate=cost(4 * work * outs, 0, 4 * work),
            name="apply_tile",
        )(sums, scalars, z, p, z_other, p_other, tile)

    def back(u, tile, half, count):
        return pl.pallas_call(
            functools.partial(back_kernel, half, count),
            grid=(grid[0] // MERGE,),
            in_specs=[whole(u.shape), tiles],
            out_specs=pl.BlockSpec((MERGE * GROUP, outs + RIDE, LANES), lambda i: (i, 0, 0)),
            out_shape=jax.ShapeDtypeStruct((n_ctr, outs + RIDE, LANES), F32),
            scratch_shapes=[pltpu.VMEM((outs, n_pts), BF), pltpu.VMEM((RIDE, LANES), F32)] + copies(1),
            compiler_params=PARAMS,
            cost_estimate=cost(2 * work * outs, 0, 2 * work),
            name="back_tile",
        )(u, tile)

    def reduce_points(u, rows):
        u = jnp.sum(exchange(u, "z"), axis=0).astype(BF)
        return spread(jnp.concatenate([u, pack(rows)], 0) if rows else u, "z")

    def reduce_centres(u, tile, count):
        v = other_core(back(u, tile, 1, count))
        v = back(u, tile, 0, count) + v
        return exchange(v, "ctr")

    def local(kernel, shapes, *operands):
        return pl.pallas_call(
            functools.partial(kernel, float(total_points)),
            out_shape=[jax.ShapeDtypeStruct(shape, F32) for shape in shapes],
            compiler_params=SMALL,
            cost_estimate=cost(2 * n_ctr * outs * LANES, 0, 4 * n_ctr * outs * LANES),
            name=kernel.__name__,
        )(*operands)

    def lanes(left, right):
        return jnp.sum(left * right, axis=0)

    mine = lax.dynamic_slice_in_dim(points, lax.axis_index("ctr") * share, share, 0)
    pts = spread(mine, "z").reshape(n_pts, dim)
    p0 = direction.T
    parts = pl.pallas_call(
        start_kernel,
        in_specs=[pl.BlockSpec(memory_space=pltpu.HBM)] * 2,
        out_shape=jax.ShapeDtypeStruct((n_ctr, LANES + 2 * outs, dim), BF),
        scratch_shapes=[pltpu.VMEM(centres.shape, BF), pltpu.VMEM(p0.shape, F32), pltpu.SemaphoreType.DMA((2,))],
        compiler_params=SMALL,
        name="start_kernel",
    )(centres, p0)
    own = exchange(parts, "ctr")
    other = other_core(own)

    tile, u0 = build(pts, own, other)
    z0 = precondition(factor, residual)
    u0 = reduce_points(u0, [lanes(residual.T, z0.T), lanes(p0, p0)])
    v0 = reduce_centres(u0, tile, 2)
    r1, scalars = local(first_kernel, [p0.shape, (RIDE, LANES)], v0, p0, residual.T)
    z1 = precondition(factor, r1.T).T
    zeros = [jnp.zeros((LANES,), F32)] * (RIDE - 3)
    block = jnp.stack([lanes(r1, z1), lanes(z1, z1), lanes(z1, p0)] + zeros)
    block = block + other_core(block)
    own_z = spread(jnp.concatenate([z1, block], 0), "ctr")
    other_z = other_core(own_z)
    sums = spread(jnp.sum(own_z[:, outs:], axis=0), "z")
    u1 = apply(sums, scalars, own_z, own, other_z, other, tile)
    u1 = reduce_points(u1, [])
    v1 = reduce_centres(u1, tile, 0)
    x2, r2 = local(last_kernel, [p0.shape, p0.shape], v1, sums, scalars, z1, p0, r1, solution.T)
    return x2.T, r2.T


def solution(mesh):
    shape = (mesh.shape["pt"] // CORES, CORES, mesh.shape["ctr"])
    fine = Mesh(mesh.devices.reshape(shape), ("z", "core", "ctr"))
    rows = P(("z", "core", "ctr"), None)
    return jax.shard_map(
        body,
        mesh=fine,
        in_specs=(P(("z", "core"), None),) + (rows,) * 5,
        out_specs=(rows, rows),
        check_vma=False,
    )
```

```python
import functools
import math

import jax
import jax.numpy as jnp
from jax import lax
from jax.experimental import pallas as pl
from jax.experimental.pallas import tpu as pltpu
from jax.sharding import Mesh, PartitionSpec as P

GAMMA_SCALE = 0.8
RIDGE = 64.0
CORES = 2
LANES = 128
GROUP = 2
MERGE = 2
ROWS = 16
RIDE = 8
BF = jnp.bfloat16
F32 = jnp.float32
SMALL = pltpu.CompilerParams(vmem_limit_bytes=8 * 1024 * 1024)
PARAMS = pltpu.CompilerParams(vmem_limit_bytes=50 * 1024 * 1024)


def precondition(factor, resid):
    lower = lax.linalg.triangular_solve(factor, resid, left_side=True, lower=True)
    return lax.linalg.triangular_solve(factor, lower, left_side=True, lower=True, transpose_a=True)


def exchange(blocks, axes):
    return lax.all_to_all(blocks, axes, 0, 0, tiled=True)


def spread(block, axes):
    count = lax.axis_size(axes)
    return exchange(jnp.broadcast_to(block[None], (count,) + block.shape), axes)


def other_core(block):
    return lax.ppermute(block, "core", [(0, 1), (1, 0)])


def pack(rows):
    pieces = []
    for row in rows:
        for _ in range(3):
            piece = lax.reduce_precision(row, 8, 7)
            pieces.append(piece)
            row = row - piece
    pieces += [jnp.zeros_like(pieces[0])] * (ROWS - len(pieces))
    return jnp.stack(pieces).astype(BF)


def chunks_of(total):
    half = total.shape[0] // 2
    return [
        total[part * half : (part + 1) * half, at : at + LANES]
        for at in range(0, total.shape[1], LANES)
        for part in range(2)
    ]


def add_up(step, part, u_ref, acc):
    @pl.when(step == 0)
    def _():
        acc[...] = part

    @pl.when(step > 0)
    def _():
        acc[...] += part

    @pl.when(step == pl.num_programs(0) - 1)
    def _():
        for at, piece in enumerate(chunks_of(acc[...])):
            u_ref[at] = piece


def rows_at(step):
    rows = GROUP * LANES
    return pl.ds(pl.multiple_of(step * rows, rows), rows)


def tile_copy(source, target, sems, step):
    rows = rows_at(step)
    return pltpu.make_async_copy(source.at[rows], target.at[rows], sems.at[step])


def fetch(steps, order, tile_ref, buf, sems):
    @pl.when(pl.program_id(0) == 0)
    def _():
        for at in order:
            tile_copy(tile_ref, buf, sems, at).start()

    for step in steps:
        tile_copy(tile_ref, buf, sems, step).wait()
    return [buf[rows_at(step)] for step in steps]


def gap_columns(rows, place):
    wide = rows.astype(F32)
    left = 0.5 * (rows.shape[1] - jnp.sum(wide * wide, axis=1, keepdims=True))
    lane = lax.broadcasted_iota(jnp.int32, (rows.shape[0], LANES), 1)
    columns = jnp.where(lane < 6, 1.0, 0.0)
    for k in range(3):
        piece = left.astype(BF).astype(F32)
        columns = jnp.where(lane == place + k, piece, columns)
        left = left - piece
    return columns.astype(BF)


def start_kernel(cen_hbm, p_hbm, out_ref, cen_ref, p_ref, sems):
    dim, outs = cen_ref.shape[0], p_ref.shape[0]
    reads = [pltpu.make_async_copy(cen_hbm, cen_ref, sems.at[0]), pltpu.make_async_copy(p_hbm, p_ref, sems.at[1])]
    for read in reads:
        read.start()
    for read in reads:
        read.wait()
    high = p_ref[...].astype(BF)
    low = (p_ref[...] - high.astype(F32)).astype(BF)
    for k in range(out_ref.shape[0]):
        out_ref[k, :dim] = cen_ref[...]
        out_ref[k, dim : dim + outs] = high
        out_ref[k, dim + outs :] = low


def build_kernel(gamma, pts_ref, own_ref, other_ref, tile_ref, u_ref, acc, buf, sems, side):
    step = pl.program_id(0)
    steps = pl.num_programs(0)
    outs = acc.shape[0]

    @pl.when(step == 0)
    def _():
        side[...] = gap_columns(pts_ref[...], 3)

    pts = jnp.concatenate([pts_ref[...], side[...]], axis=1)
    part = None
    for blk_ref, first in ((own_ref, step), (other_ref, step + steps)):
        for m in range(MERGE):
            blks = [blk_ref[g] for g in range(m * GROUP, (m + 1) * GROUP)]
            place = MERGE * first + m
            cen = jnp.concatenate([blk[:LANES] for blk in blks], axis=0)
            vec = jnp.concatenate([blk[LANES : LANES + outs] for blk in blks], axis=1)
            cen = jnp.concatenate([cen, gap_columns(cen, 0)], axis=1)
            cross = lax.dot_general(cen, pts, (((1,), (1,)), ((), ())), preferred_element_type=F32)
            tile = jnp.exp2((2.0 * gamma * math.log2(math.e)) * cross).astype(BF)
            buf[rows_at(place)] = tile
            tile_copy(buf, tile_ref, sems, place).start()
            term = jnp.dot(vec, tile, preferred_element_type=F32)
            part = term if part is None else part + term
    add_up(step, part, u_ref, acc)

    @pl.when(step == steps - 1)
    def _():
        for at in range(sems.shape[0]):
            tile_copy(buf, tile_ref, sems, at).wait()


def apply_kernel(sums_ref, scalars_ref, z_ref, p_ref, z_other_ref, p_other_ref, tile_ref, u_ref, acc, buf, sems, beta):
    step = pl.program_id(0)
    outs = acc.shape[0]
    count = sems.shape[0] // (2 * MERGE)

    def groups(at):
        return [MERGE * first + m for first in (at, at + count) for m in range(MERGE)]

    order = [group for at in range(count) for group in groups(at)]
    tiles = fetch(groups(step), order, tile_ref, buf, sems)

    @pl.when(step == 0)
    def _():
        rate = totals(sums_ref)[0:1] / scalars_ref[0:1, 0:1]
        beta[...] = jnp.broadcast_to(rate, beta.shape)

    part = None
    for tile, z, p in ((tiles[:MERGE], z_ref, p_ref), (tiles[MERGE:], z_other_ref, p_other_ref)):
        for m in range(MERGE):
            vec = []
            for g in range(m * GROUP, (m + 1) * GROUP):
                vec.append((z[g, :outs] + beta[...] * (p[g, :outs].astype(F32) + p[g, outs:].astype(F32))).astype(BF))
            term = jnp.dot(jnp.concatenate(vec, axis=1), tile[m], preferred_element_type=F32)
            part = term if part is None else part + term
    add_up(step, part, u_ref, acc)


def back_kernel(half, count, u_ref, tile_ref, v_ref, ub, ride, buf, sems):
    rows = buf.shape[0]
    outs = ub.shape[0]
    step = pl.program_id(0)
    mine = [MERGE * step + m for m in range(MERGE)]
    tiles = fetch(mine, range(sems.shape[0]), tile_ref.at[pl.ds(half * rows, rows)], buf, sems)
    half = outs // 2

    @pl.when(step == 0)
    def _():
        squares = jnp.zeros((half, LANES), F32)
        for at in range(u_ref.shape[0]):
            piece = u_ref[at, :half]
            low = (at % 2) * half
            ub[low : low + half, (at // 2) * LANES : (at // 2 + 1) * LANES] = piece
            squares += piece.astype(F32) * piece.astype(F32)
        packed = jnp.sum(u_ref[:, half:].astype(F32), axis=0) if count else None
        rows = [packed[3 * k : 3 * k + 1] + packed[3 * k + 1 : 3 * k + 2] + packed[3 * k + 2 : 3 * k + 3] for k in range(count)]
        rows.append(jnp.sum(squares, axis=0, keepdims=True))
        rows.append(jnp.zeros((RIDE - count - 1, LANES), F32))
        ride[...] = jnp.concatenate(rows, axis=0)

    for m, tile in enumerate(tiles):
        v = lax.dot_general(ub[...], tile, (((1,), (1,)), ((), ())), preferred_element_type=F32)
        for g in range(GROUP):
            v_ref[m * GROUP + g, :outs] = v[:, g * LANES : (g + 1) * LANES]
            v_ref[m * GROUP + g, outs:] = ride[...]


def totals(sums_ref):
    return jnp.sum(jnp.sum(sums_ref[...], axis=0), axis=1, keepdims=True)


def first_kernel(points, v_ref, p_ref, r_ref, r1_ref, scalars_ref):
    outs = p_ref.shape[0]
    v = jnp.sum(v_ref[...], axis=0)
    s = jnp.sum(v[outs:], axis=1, keepdims=True)
    alpha = s[0:1] / (s[2:3] / points + RIDGE * s[1:2])
    r1_ref[...] = r_ref[...] - alpha * (v[:outs] / points + RIDGE * p_ref[...])
    rows = [jnp.broadcast_to(value, (1, LANES)) for value in (s[0:1], s[1:2], alpha)]
    scalars_ref[...] = jnp.concatenate(rows + [jnp.zeros((RIDE - 3, LANES), F32)], axis=0)


def last_kernel(points, v_ref, sums_ref, scalars_ref, z_ref, p_ref, r_ref, x_ref, x_out, r_out):
    outs = p_ref.shape[0]
    v = jnp.sum(v_ref[...], axis=0)
    uu = jnp.sum(v[outs : outs + 1], axis=1, keepdims=True)
    t = totals(sums_ref)
    rz0, pp0, alpha0 = [scalars_ref[k : k + 1, 0:1] for k in range(3)]
    beta = t[0:1] / rz0
    p1 = z_ref[...] + beta * p_ref[...]
    pp = t[1:2] + beta * (2.0 * t[2:3] + beta * pp0)
    alpha1 = t[0:1] / (uu / points + RIDGE * pp)
    x_out[...] = x_ref[...] + alpha0 * p_ref[...] + alpha1 * p1
    r_out[...] = r_ref[...] - alpha1 * (v[:outs] / points + RIDGE * p1)


def body(points, centres, factor, solution, residual, direction):
    dim = points.shape[1]
    gamma = GAMMA_SCALE / math.sqrt(dim)
    outs = direction.shape[1]
    n_z, n_ctr = lax.axis_size("z"), lax.axis_size("ctr")
    total_points = points.shape[0] * n_z * CORES
    n_pts = points.shape[0]
    share = n_pts // n_ctr
    grid = (n_ctr // GROUP,)
    u_shape = jax.ShapeDtypeStruct((2 * n_pts // LANES, outs // 2, LANES), F32)
    whole = lambda shape: pl.BlockSpec(shape, lambda i: (0,) * len(shape))
    tiles = pl.BlockSpec(memory_space=pltpu.HBM)

    def copies(halves):
        return [pltpu.VMEM((halves * n_ctr * LANES, n_pts), BF), pltpu.SemaphoreType.DMA((halves * grid[0],))]
    acc = pltpu.VMEM((outs, n_pts), F32)
    work = n_ctr * LANES * n_pts

    def cost(flops, exps, size):
        return pl.CostEstimate(flops=flops, transcendentals=exps, bytes_accessed=size)

    def build(pts, own, other):
        return pl.pallas_call(
            functools.partial(build_kernel, gamma),
            grid=(grid[0] // MERGE,),
            in_specs=[whole(pts.shape)] + [pl.BlockSpec((MERGE * GROUP, own.shape[1], LANES), lambda i: (i, 0, 0))] * 2,
            out_specs=[tiles, whole(u_shape.shape)],
            out_shape=[jax.ShapeDtypeStruct((CORES * n_ctr * LANES, n_pts), BF), u_shape],
            scratch_shapes=[acc] + copies(CORES) + [pltpu.VMEM((n_pts, LANES), BF)],
            compiler_params=PARAMS,
            cost_estimate=cost(4 * work * (dim + outs), 2 * work, 4 * work),
            name="build_tile",
        )(pts, own, other)

    def apply(sums, scalars, z, p, z_other, p_other, tile):
        step_z = pl.BlockSpec((MERGE * GROUP, z.shape[1], LANES), lambda i: (i, 0, 0))
        step_p = pl.BlockSpec((MERGE * GROUP, 2 * outs, LANES), lambda i: (i, 1, 0))
        return pl.pallas_call(
            apply_kernel,
            grid=(grid[0] // MERGE,),
            in_specs=[whole(sums.shape), whole(scalars.shape)] + [step_z, step_p] * 2 + [tiles],
            out_specs=whole(u_shape.shape),
            out_shape=u_shape,
            scratch_shapes=[acc] + copies(CORES) + [pltpu.VMEM((1, LANES), F32)],
            compiler_params=PARAMS,
            cost_estimate=cost(4 * work * outs, 0, 4 * work),
            name="apply_tile",
        )(sums, scalars, z, p, z_other, p_other, tile)

    def back(u, tile, half, count):
        return pl.pallas_call(
            functools.partial(back_kernel, half, count),
            grid=(grid[0] // MERGE,),
            in_specs=[whole(u.shape), tiles],
            out_specs=pl.BlockSpec((MERGE * GROUP, outs + RIDE, LANES), lambda i: (i, 0, 0)),
            out_shape=jax.ShapeDtypeStruct((n_ctr, outs + RIDE, LANES), F32),
            scratch_shapes=[pltpu.VMEM((outs, n_pts), BF), pltpu.VMEM((RIDE, LANES), F32)] + copies(1),
            compiler_params=PARAMS,
            cost_estimate=cost(2 * work * outs, 0, 2 * work),
            name="back_tile",
        )(u, tile)

    def reduce_points(u, rows):
        u = jnp.sum(exchange(u, "z"), axis=0).astype(BF)
        return spread(jnp.concatenate([u, pack(rows)], 0) if rows else u, "z")

    def reduce_centres(u, tile, count):
        v = other_core(back(u, tile, 1, count))
        v = back(u, tile, 0, count) + v
        return exchange(v, "ctr")

    def local(kernel, shapes, *operands):
        return pl.pallas_call(
            functools.partial(kernel, float(total_points)),
            out_shape=[jax.ShapeDtypeStruct(shape, F32) for shape in shapes],
            compiler_params=SMALL,
            cost_estimate=cost(2 * n_ctr * outs * LANES, 0, 4 * n_ctr * outs * LANES),
            name=kernel.__name__,
        )(*operands)

    def lanes(left, right):
        return jnp.sum(left * right, axis=0)

    mine = lax.dynamic_slice_in_dim(points, lax.axis_index("ctr") * share, share, 0)
    pts = spread(mine, "z").reshape(n_pts, dim)
    p0 = direction.T
    parts = pl.pallas_call(
        start_kernel,
        in_specs=[pl.BlockSpec(memory_space=pltpu.HBM)] * 2,
        out_shape=jax.ShapeDtypeStruct((n_ctr, LANES + 2 * outs, dim), BF),
        scratch_shapes=[pltpu.VMEM(centres.shape, BF), pltpu.VMEM(p0.shape, F32), pltpu.SemaphoreType.DMA((2,))],
        compiler_params=pltpu.CompilerParams(vmem_limit_bytes=62 * 1024 * 1024),
        name="start_kernel",
    )(centres, p0)
    own = exchange(parts, "ctr")
    other = other_core(own)

    tile, u0 = build(pts, own, other)
    z0 = precondition(factor, residual)
    u0 = reduce_points(u0, [lanes(residual.T, z0.T), lanes(p0, p0)])
    v0 = reduce_centres(u0, tile, 2)
    r1, scalars = local(first_kernel, [p0.shape, (RIDE, LANES)], v0, p0, residual.T)
    z1 = precondition(factor, r1.T).T
    zeros = [jnp.zeros((LANES,), F32)] * (RIDE - 3)
    block = jnp.stack([lanes(r1, z1), lanes(z1, z1), lanes(z1, p0)] + zeros)
    block = block + other_core(block)
    own_z = spread(jnp.concatenate([z1, block], 0), "ctr")
    other_z = other_core(own_z)
    sums = spread(jnp.sum(own_z[:, outs:], axis=0), "z")
    u1 = apply(sums, scalars, own_z, own, other_z, other, tile)
    u1 = reduce_points(u1, [])
    v1 = reduce_centres(u1, tile, 0)
    x2, r2 = local(last_kernel, [p0.shape, p0.shape], v1, sums, scalars, z1, p0, r1, solution.T)
    return x2.T, r2.T


def solution(mesh):
    shape = (mesh.shape["pt"] // CORES, CORES, mesh.shape["ctr"])
    fine = Mesh(mesh.devices.reshape(shape), ("z", "core", "ctr"))
    rows = P(("z", "core", "ctr"), None)
    return jax.shard_map(
        body,
        mesh=fine,
        in_specs=(P(("z", "core"), None),) + (rows,) * 5,
        out_specs=(rows, rows),
        check_vma=False,
    )
```
